256 devices in a mesh: rep: 16 (over z, core), fsdp: 16 (over x, y).
Axes of the slice: x: 4, y: 4, z: 8, core: 2. Of those that a mesh axis runs over, the one named last changes fastest.
Arguments:
- tokens: bfloat16 [512, 128, 8192], P('rep', 'fsdp'), may hold values from -6 to 6
- cotangent: bfloat16 [512, 128, 1024], P('rep', 'fsdp'), may hold values from -6 to 6
- frozen_weight: bfloat16 [8192, 1024], P('fsdp'), may hold values from -0.0625 to 0.0625
- down_factor_table: bfloat16 [32, 64, 8192], P('rep', None, 'fsdp'), may hold values from -0.0625 to 0.0625
- up_factor_table: bfloat16 [32, 64, 1024], P('rep', 'fsdp'), may hold values from -0.09375 to 0.09375
- adapter_of_block: int32 [512], P('rep'), may hold values from 0 to 31, as said below
- block_destination: int32 [512], P('rep'), may hold values from 0 to 511, as said below
- adapter_table_row: int32 [32], replicated, may hold values from 0 to 31, as said below
Outputs:
- values: bfloat16 [512, 128, 1024], P('rep', 'fsdp')
- token_grad: bfloat16 [512, 128, 8192], P('rep', 'fsdp')
- down_gradient: float32 [32, 64, 8192], P('rep', None, 'fsdp')
- up_gradient: float32 [32, 64, 1024], P('rep', 'fsdp')
The draws below stay inside these ranges and needn't reach their ends.
Inputs may be any that keep to these rules, and one draw needn't show every extreme that they name: A permutation of the 512 blocks: block b moves to place block_destination[b], on replica block_destination[b] // 32. Of the blocks of one replica at most 2 go to any one replica, and in every draw some replica sends exactly 2 blocks to some replica. A permutation of the adapters. Adapter a's factors and gradients are row adapter_table_row[a] of the tables, and replica adapter_table_row[a] // 2 owns them. Every block's adapter is owned by the replica that the block moves to: adapter_table_row[adapter_of_block[b]] // 2 == block_destination[b] // 32.
All inputs are finite; a program needn't handle non-finite values.
Results may differ from the reference program's by a relative error of at most 0.001.
Values may be sent and summed in bfloat16 or wider, within the bound.
A program may use at most 128 MiB of HBM per device.

```python
import jax
import jax.numpy as jnp
from jax import lax

MODEL_WIDTH = 8192
VALUE_HEADS_WIDTH = 1024
ADAPTER_RANK = 64
BT = 128
ADP_REP = 2
BPR = 32
BLOCKS = 512
CAP = 2
ADAPTER_COUNT = 32
N_REP = 16


def plan_tables(key):
    keys = jax.random.split(key, 9)
    dest_order = jax.random.permutation(keys[0], N_REP)
    source_order = jax.random.permutation(keys[1], N_REP)
    offsets = jax.random.permutation(keys[2], N_REP)
    slot_rank = jax.vmap(lambda k: jax.random.permutation(k, BPR))(jax.random.split(keys[3], N_REP))
    arrive_perm = jax.vmap(lambda k: jax.random.permutation(k, BPR))(jax.random.split(keys[4], N_REP))
    group_index = slot_rank // CAP
    dest_rep = dest_order[(source_order[:, None] + offsets[group_index]) % N_REP]
    dest_slot = arrive_perm[dest_rep, slot_rank]
    block_destination = (dest_rep * BPR + dest_slot).reshape(-1).astype(jnp.int32)
    adapter_table_row = jax.random.permutation(keys[5], ADAPTER_COUNT).astype(jnp.int32)
    owner_id = jnp.argsort(adapter_table_row).astype(jnp.int32)
    threshold = jax.random.randint(keys[6], (N_REP,), 10, 91)
    coin_draw = jax.random.randint(keys[7], (N_REP, BPR), 0, 100)
    other_pick = jax.random.randint(keys[8], (N_REP, BPR), 1, max(ADP_REP, 2))
    other_pick = jnp.minimum(other_pick, ADP_REP - 1)
    local_pick = jnp.where(coin_draw < threshold[dest_rep], 0, other_pick)
    adapter_of_block = owner_id[dest_rep * ADP_REP + local_pick].reshape(-1).astype(jnp.int32)
    return (block_destination, adapter_of_block, adapter_table_row)


def draw_block_destination(key, part):
    return plan_tables(key)[0]


def draw_adapter_of_block(key, part):
    return plan_tables(key)[1]


def draw_adapter_table_row(key, part):
    return plan_tables(key)[2]


def block_scale(rng, shape, shards, least, top_value):
    level, own = 1.0, jax.random.fold_in(rng, 6)
    for dim, parts in shards:
        heights = jnp.exp(jax.random.uniform(jax.random.fold_in(own, dim), (parts,), jnp.float32, least / len(shards), top_value / len(shards)))
        level = level * jnp.repeat(heights, shape[dim] // parts).reshape([-1 if axis == dim else 1 for axis in range(len(shape))])
    return level


def bell_draw(stream_key, shape, spread, most, pieces=(), kind=jnp.bfloat16):
    result = jax.random.normal(stream_key, shape, jnp.float32) * spread
    if len(pieces) > 0:
        result = block_scale(stream_key, shape, pieces, -0.22, 0.18) * result
    return jnp.clip(result, min=-most, max=most).astype(kind)


def setup_inputs(seed: int = 0) -> dict:
    splits = jax.random.split(jax.random.key(seed), 9)
    tokens = bell_draw(splits[0], (BLOCKS, BT, MODEL_WIDTH), 1.0, 6.0, ((0, 16), (1, 16)))
    cotangent = bell_draw(splits[1], (BLOCKS, BT, VALUE_HEADS_WIDTH), 1.0, 6.0, ((0, 16), (1, 16)))
    frozen_weight = bell_draw(splits[2], (MODEL_WIDTH, VALUE_HEADS_WIDTH), MODEL_WIDTH ** -0.5, 0.0625, ((0, 16),))
    down_factor_table = bell_draw(splits[3], (ADAPTER_COUNT, ADAPTER_RANK, MODEL_WIDTH), MODEL_WIDTH ** -0.5, 0.0625, ((0, 16), (2, 16)))
    up_factor_table = bell_draw(splits[4], (ADAPTER_COUNT, ADAPTER_RANK, VALUE_HEADS_WIDTH), (ADAPTER_RANK * ADAPTER_RANK) ** -0.5, 0.09375, ((0, 16), (1, 16)))
    adapter_of_block = draw_adapter_of_block(jax.random.fold_in(splits[8], 71), 0)
    block_destination = draw_block_destination(jax.random.fold_in(splits[8], 71), 0)
    adapter_table_row = draw_adapter_table_row(jax.random.fold_in(splits[8], 71), 0)
    return dict(tokens=tokens, cotangent=cotangent, frozen_weight=frozen_weight, down_factor_table=down_factor_table, up_factor_table=up_factor_table, adapter_of_block=adapter_of_block, block_destination=block_destination, adapter_table_row=adapter_table_row)


lowrank_multiplier = 2.0
highest = lax.Precision.HIGHEST


def reference(tokens, cotangent, frozen_weight, down_factor_table, up_factor_table, adapter_of_block, block_destination, adapter_table_row):
    shipped_sequence_items = jnp.zeros_like(tokens).at[block_destination].set(tokens)
    source_rows = jnp.take(adapter_table_row, adapter_of_block, axis=0).astype(jnp.int32)
    moved_rows = jnp.zeros((BLOCKS,), jnp.int32).at[block_destination].set(source_rows)

    def scan_replica(carry, inputs):
        lowering_grad_accumulated, up_gradient_sum = carry
        block_tokens, block_cot, rows_per_block = inputs
        shrinking_operand_entries = jnp.take(down_factor_table, rows_per_block, axis=0).astype(jnp.float32)
        expanding_operand_entries = jnp.take(up_factor_table, rows_per_block, axis=0).astype(jnp.float32)
        sequence_item_real = block_tokens.astype(jnp.float32)
        upstream_derivative_lone = block_cot.astype(jnp.float32)
        adapter_middle = jnp.einsum("zfw,zgw->zfg", sequence_item_real, shrinking_operand_entries, precision=highest)
        frozen_values = jnp.dot(block_tokens.reshape(BPR * BT, MODEL_WIDTH), frozen_weight,
                              preferred_element_type=jnp.float32).reshape(BPR, BT, VALUE_HEADS_WIDTH)
        values = (frozen_values + lowrank_multiplier * jnp.einsum("uqj,ujp->uqp", adapter_middle, expanding_operand_entries, precision=highest)).astype(jnp.bfloat16)
        lowrank_derivative_sweep = jnp.einsum("rho,rbo->rhb", upstream_derivative_lone, expanding_operand_entries, precision=highest)
        fixed_weights_derivative = jnp.dot(block_cot.reshape(BPR * BT, VALUE_HEADS_WIDTH), frozen_weight.T,
                            preferred_element_type=jnp.float32).reshape(BPR, BT, MODEL_WIDTH)
        shipped_derivative = (fixed_weights_derivative + lowrank_multiplier * jnp.einsum("xft,xtg->xfg", lowrank_derivative_sweep, shrinking_operand_entries, precision=highest)).astype(jnp.bfloat16)
        adapter_matches = (rows_per_block[:, None] == jnp.arange(ADAPTER_COUNT, dtype=jnp.int32)[None, :]).astype(jnp.float32)
        tokenset_shrinking_operand = jnp.einsum("qty,qtw->qyw", lowrank_derivative_sweep, sequence_item_real, precision=highest)
        block_up_factor = jnp.einsum("zaw,zay->zwy", adapter_middle, upstream_derivative_lone, precision=highest)
        lowering_grad_accumulated = lowering_grad_accumulated + lowrank_multiplier * jnp.einsum("af,aqv->fqv", adapter_matches, tokenset_shrinking_operand, precision=highest)
        up_gradient_sum = up_gradient_sum + lowrank_multiplier * jnp.einsum("pl,pzx->lzx", adapter_matches, block_up_factor, precision=highest)
        return (lowering_grad_accumulated, up_gradient_sum), (values, shipped_derivative)

    start_a = jnp.zeros((ADAPTER_COUNT, ADAPTER_RANK, MODEL_WIDTH), jnp.float32)
    start_b = jnp.zeros((ADAPTER_COUNT, ADAPTER_RANK, VALUE_HEADS_WIDTH), jnp.float32)
    inputs = (shipped_sequence_items.reshape(N_REP, BPR, BT, MODEL_WIDTH), cotangent.reshape(N_REP, BPR, BT, VALUE_HEADS_WIDTH),
              moved_rows.reshape(N_REP, BPR))
    (down_gradient, up_gradient), (values, shipped_derivative) = lax.scan(scan_replica, (start_a, start_b), inputs)
    values = values.reshape(BLOCKS, BT, VALUE_HEADS_WIDTH)
    shipped_derivative = shipped_derivative.reshape(BLOCKS, BT, MODEL_WIDTH)
    token_grad = jnp.take(shipped_derivative, block_destination, axis=0)
    return values, token_grad, down_gradient, up_gradient
```

```python
import functools

import jax
import jax.numpy as jnp
import numpy as np
from jax import lax
from jax.experimental import pallas as pl
from jax.experimental.pallas import tpu as pltpu
from jax.sharding import PartitionSpec as P

MESH = pl.DeviceIdType.MESH
bf16, f32 = jnp.bfloat16, jnp.float32

NR = 16
NF = 16
T = 256
RT = T // NR
D = 8192
V = 1024
DS = D // NF
HALF = DS // 2
A = 128
G = 4
GC = D // G

PLANE = [(i % 4, (i + i // 4) % 4) for i in range(1, 16)]
REPS = [(dz, dc) for dz in (4, 3, 5, 2, 6, 1, 7) for dc in (0, 1)] + [(0, 1)]


def nt(a, b):
    return lax.dot_general(a, b, (((1,), (1,)), ((), ())), preferred_element_type=f32)


def nn(a, b):
    return jnp.dot(a, b, preferred_element_type=f32)


def split(v):
    hi = v.astype(bf16)
    return hi, (v - hi.astype(f32)).astype(bf16)


def kernel(
    tok, cot, w, down, up, sel, selt, lab, q,
    tg, val, dg, ug,
    xs, xr, gs, gr, wf, dn, upr, labr, dpart, drecv, upart, urecv, cotp, gcat, gtcat, upb, acc, mid,
    tok_sem, x_send, x_recv, lab_sem, dn_sem, up_sem, w_own, w_send, w_recv, sib_send, sib_recv,
    g_send, g_recv, r_sem, u_sem, out_sem,
):
    rep, fs = lax.axis_index("rep"), lax.axis_index("fsdp")
    z, c, x, y = rep // 2, rep % 2, fs // 4, fs % 4
    plane = [((x + dx) % 4) * 4 + (y + dy) % 4 for dx, dy in PLANE]
    reps = [((z + dz) % 8) * 2 + (c + dc) % 2 for dz, dc in REPS]
    sib = rep + 1 - 2 * c

    barrier = pltpu.get_barrier_semaphore()
    for r in reps:
        pl.semaphore_signal(barrier, inc=1, device_id=(r, fs), device_id_type=MESH)
    for f in plane:
        pl.semaphore_signal(barrier, inc=1, device_id=(rep, f), device_id_type=MESH)

    def group(g):
        return pl.ds(pl.multiple_of(g * GC, GC), GC)

    def loads(g):
        return pltpu.make_async_copy(tok.at[:, group(g)], gs.at[:, group(g)], tok_sem.at[g])

    for g in range(G):
        loads(g).start()
    pl.semaphore_wait(barrier, len(reps) + len(plane))

    def rows(r):
        return pl.ds(pl.multiple_of(r * RT, RT), RT)

    def push(src, dst, send, recv, r, f):
        pltpu.make_async_remote_copy(
            src_ref=src, dst_ref=dst, send_sem=send, recv_sem=recv,
            device_id=(r, f), device_id_type=MESH,
        ).start()

    def done(ref, sem):
        pltpu.make_async_copy(ref, ref, sem).wait()

    for r in reps:
        push(lab.at[rows(r)], labr.at[rows(rep)], lab_sem.at[0], lab_sem.at[1], r, fs)
    pltpu.make_async_copy(lab.at[rows(rep)], labr.at[rows(rep)], lab_sem.at[1]).start()
    mine8 = pl.ds(pl.multiple_of(fs * 8, 8), 8)
    for f in plane:
        push(up, upr.at[mine8], up_sem.at[0], up_sem.at[1], rep, f)
    pltpu.make_async_copy(up, upr.at[mine8], up_sem.at[1]).start()
    for f in plane:
        push(down, dn.at[fs], dn_sem.at[0], dn_sem.at[1], rep, f)
    pltpu.make_async_copy(down, dn.at[fs], dn_sem.at[1]).start()

    def wrows(f, h):
        return pl.ds(pl.multiple_of(f * DS + h * HALF, HALF), HALF)

    my_half = pl.ds(pl.multiple_of(c * HALF, HALF), HALF)
    for f in plane:
        push(w.at[my_half], wf.at[wrows(fs, c)], w_send, w_recv.at[fs], rep, f)
    own_w = pltpu.make_async_copy(w, wf.at[pl.ds(pl.multiple_of(fs * DS, DS), DS)], w_own)
    own_w.start()

    for g in range(G):
        loads(g).wait()
        for k in range(GC // 512):
            cols = pl.ds(g * GC + k * 512, 512)
            xs[:, cols] = nn(sel[...], gs[:, cols]).astype(bf16)
        for r in reps:
            push(xs.at[rows(r), group(g)], xr.at[rows(rep), group(g)], x_send.at[g], x_recv.at[g], r, fs)
        pltpu.make_async_copy(
            xs.at[rows(rep), group(g)], xr.at[rows(rep), group(g)], x_recv.at[g]
        ).start()

    done(labr, lab_sem.at[1])
    cotp[...] = nn(labr[:, :T], cot[...]).astype(bf16)
    done(upr, up_sem.at[1])
    upb[...] = nn(q[...], upr[...].astype(bf16)).astype(bf16)
    mask = labr[:, T:].astype(f32)
    back = 2.0 * nt(cotp[...], upb[...]) * mask
    hi, lo = split(back)
    gcat[:, :A] = hi
    gcat[:, A:] = lo
    hi, lo = split(back.T)
    gtcat[:A, :] = hi
    gtcat[A:, :] = lo
    done(dn, dn_sem.at[1])

    def dcols(f):
        return pl.ds(pl.multiple_of(f * DS, DS), DS)

    def grads(f):
        wv = wf[dcols(f), :]
        dv = dn[f]
        out = nt(cotp[...], wv)
        out = out + nn(gcat[:, :A], dv) + nn(gcat[:, A:], dv)
        gs[:, dcols(f)] = out.astype(bf16)
        for r in reps:
            push(gs.at[rows(r), dcols(f)], gr.at[rows(rep), dcols(f)], g_send.at[f], g_recv.at[f], r, fs)
        pltpu.make_async_copy(
            gs.at[rows(rep), dcols(f)], gr.at[rows(rep), dcols(f)], g_recv.at[f]
        ).start()

    own_w.wait()
    grads(fs)

    def from_offset(i):
        return ((x + 4 - i % 4) % 4) * 4 + (y + 8 - (i + i // 4) % 4) % 4

    def forward_half(i):
        f = from_offset(i)
        done(wf.at[wrows(f, c)], w_recv.at[f])
        push(wf.at[wrows(f, c)], wf.at[wrows(f, c)], sib_send, sib_recv.at[f], sib, fs)

    forward_half(1)

    def step(i, _):
        @pl.when(i < 15)
        def _():
            forward_half(i + 1)

        f = from_offset(i)
        done(wf.at[wrows(f, 1 - c)], sib_recv.at[f])
        grads(f)
        return 0

    lax.fori_loop(1, 16, step, 0)

    acc[...] = jnp.zeros_like(acc)
    mid[...] = jnp.zeros_like(mid)

    def fwd_group(g, _):
        done(xr.at[:, group(g)], x_recv.at[g])

        def fwd(k, _):
            f = g * 4 + (y + k) % 4
            xv = xr[:, dcols(f)]
            part = nn(gtcat[...], xv)
            dpart[f] = part[:A] + part[A:]

            @pl.when(f != fs)
            def _():
                push(dpart.at[f], drecv.at[fs], r_sem.at[0], r_sem.at[1], rep, f)

            @pl.when(f == fs)
            def _():
                pltpu.make_async_copy(dpart.at[f], drecv.at[fs], r_sem.at[1]).start()

            acc[...] += nn(xv, wf[dcols(f), :])
            mid[...] += nt(xv, dn[f])
            return 0

        lax.fori_loop(0, 4, fwd, 0)
        return 0

    lax.fori_loop(0, G, fwd_group, 0)

    m2 = 2.0 * mid[...] * labr[:, T:].astype(f32)
    hi, lo = split(m2)
    out = acc[...] + nn(hi, upb[...]) + nn(lo, upb[...])
    val[...] = lax.dot_general(
        labr[:, :T], out.astype(bf16), (((0,), (0,)), ((), ())), preferred_element_type=f32
    ).astype(bf16)
    hi, lo = split(m2.T)
    hi = lax.dot_general(q[...], hi, (((0,), (0,)), ((), ())), preferred_element_type=f32).astype(bf16)
    lo = lax.dot_general(q[...], lo, (((0,), (0,)), ((), ())), preferred_element_type=f32).astype(bf16)
    upart[...] = nn(hi, cotp[...]) + nn(lo, cotp[...])
    for f in plane:
        its8 = pl.ds(pl.multiple_of(f * 8, 8), 8)
        push(upart.at[its8], urecv.at[fs], u_sem.at[0], u_sem.at[1], rep, f)
    pltpu.make_async_copy(upart.at[mine8], urecv.at[fs], u_sem.at[1]).start()

    for g in range(G):
        done(xs.at[pl.ds(0, T - RT), group(g)], x_send.at[g])

    def finish(i, _):
        f = from_offset(i)
        done(gr.at[:, dcols(f)], g_recv.at[f])
        xs[:, dcols(f)] = nn(selt[...], gr[:, dcols(f)]).astype(bf16)
        pltpu.make_async_copy(xs.at[:, dcols(f)], tg.at[:, dcols(f)], out_sem).start()
        return 0

    lax.fori_loop(0, 16, finish, 0)

    done(urecv, u_sem.at[1])
    ug[...] = jnp.sum(urecv[...], axis=0)
    done(drecv, r_sem.at[1])

    def total(k, _):
        part = pl.ds(pl.multiple_of(k * 8, 8), 8)
        out = drecv[0, part, :]
        for f in range(1, NF):
            out = out + drecv[f, part, :]
        dg[part, :] = out
        return 0

    lax.fori_loop(0, A // 8, total, 0)

    done(tg, out_sem)
    done(lab.at[pl.ds(0, T - RT)], lab_sem.at[0])
    done(upr.at[pl.ds(0, 15 * 8)], up_sem.at[0])
    done(dn.at[pl.ds(0, 15)], dn_sem.at[0])
    done(wf.at[pl.ds(0, 15 * HALF)], w_send)
    done(wf.at[pl.ds(0, 15 * HALF)], sib_send)
    done(dpart.at[pl.ds(0, 15)], r_sem.at[0])
    done(upart.at[pl.ds(0, 15 * 8)], u_sem.at[0])

    def sent(f, _):
        done(gs.at[pl.ds(0, T - RT), dcols(f)], g_send.at[f])
        return 0

    lax.fori_loop(0, 16, sent, 0)


def rank_order():
    order = np.zeros((A, A), np.float32)
    for k in range(A):
        a, r = k // 64, k % 64
        order[k, (r // 4) * 8 + a * 4 + r % 4] = 1.0
    return order


def local(
    tokens,
    cotangent,
    frozen_weight,
    down_factor_table,
    up_factor_table,
    adapter_of_block,
    block_destination,
    adapter_table_row,
):
    blocks = tokens.shape[0]
    steps = jnp.arange(blocks, dtype=jnp.int32)
    wide = jnp.arange(T, dtype=jnp.int32)
    dest_rep = block_destination // blocks
    slot = block_destination % blocks
    row = jnp.sum(
        jnp.where(adapter_of_block[:, None] == steps[None, :], adapter_table_row[None, :], 0), axis=1
    )
    adapter = row - dest_rep * 2
    before = (dest_rep[:, None] == dest_rep[None, :]) & (steps[None, :] < steps[:, None])
    place = dest_rep * 2 + jnp.sum(before.astype(jnp.int32), axis=1)
    hit = place[None, :] == steps[:, None]
    slot_at = jnp.sum(jnp.where(hit, slot[None, :], 0), axis=1)
    adapter_at = jnp.sum(jnp.where(hit, adapter[None, :], 0), axis=1)

    def by_token(v):
        return jnp.broadcast_to(v[:, None], (blocks, 8)).reshape(T)

    code = by_token(place) * 8 + wide % 8
    slot_code = by_token(slot_at) * 8 + wide % 8
    sel = (wide[:, None] == code[None, :]).astype(bf16)
    selt = (code[:, None] == wide[None, :]).astype(bf16)
    lab = jnp.concatenate(
        [
            (slot_code[:, None] == wide[None, :]).astype(bf16),
            (by_token(adapter_at)[:, None] == (wide // 64)[None, :A]).astype(bf16),
        ],
        axis=1,
    )
    q = jnp.asarray(rank_order(), bf16)

    vm = pl.BlockSpec(memory_space=pltpu.VMEM)
    hbm = pl.BlockSpec(memory_space=pl.ANY)
    dma = pltpu.SemaphoreType.DMA
    tg, val, dg, ug = pl.pallas_call(
        kernel,
        out_shape=(
            jax.ShapeDtypeStruct((T, D), bf16),
            jax.ShapeDtypeStruct((T, V), bf16),
            jax.ShapeDtypeStruct((A, DS), f32),
            jax.ShapeDtypeStruct((8, V), f32),
        ),
        in_specs=[hbm, vm, hbm, hbm, hbm, vm, vm, vm, vm],
        out_specs=(hbm, vm, vm, vm),
        scratch_shapes=[
            pltpu.VMEM((T, D), bf16),
            pltpu.VMEM((T, D), bf16),
            pltpu.VMEM((T, D), bf16),
            pltpu.VMEM((T, D), bf16),
            pltpu.VMEM((D, V), bf16),
            pltpu.VMEM((NF, A, DS), bf16),
            pltpu.VMEM((A, V), f32),
            pltpu.VMEM((T, T + A), bf16),
            pltpu.VMEM((NF, A, DS), f32),
            pltpu.VMEM((NF, A, DS), f32),
            pltpu.VMEM((A, V), f32),
            pltpu.VMEM((NF, 8, V), f32),
            pltpu.VMEM((T, V), bf16),
            pltpu.VMEM((T, 2 * A), bf16),
            pltpu.VMEM((2 * A, T), bf16),
            pltpu.VMEM((A, V), bf16),
            pltpu.VMEM((T, V), f32),
            pltpu.VMEM((T, A), f32),
            dma((G,)),
            dma((G,)),
            dma((G,)),
            dma((2,)),
            dma((2,)),
            dma((2,)),
            dma,
            dma,
            dma((NF,)),
            dma,
            dma((NF,)),
            dma((NF,)),
            dma((NF,)),
            dma((2,)),
            dma((2,)),
            dma,
        ],
        compiler_params=pltpu.CompilerParams(
            collective_id=0, has_side_effects=True, vmem_limit_bytes=60 * 1024 * 1024
        ),
        cost_estimate=pl.CostEstimate(
            flops=14 * 10**9, bytes_accessed=12 * 2**20, transcendentals=0
        ),
        name="lora_moves",
    )(
        tokens.reshape(T, D),
        cotangent.reshape(T, V),
        frozen_weight,
        down_factor_table.reshape(A, DS),
        up_factor_table.astype(f32).reshape(8, V),
        sel,
        selt,
        lab,
        q,
    )
    return (
        val.reshape(blocks, 8, V),
        tg.reshape(blocks, 8, D),
        dg.reshape(2, 64, DS),
        ug.reshape(2, 4, V),
    )


def solution(mesh):
    placed = (
        P("rep", "fsdp", None),
        P("rep", "fsdp", None),
        P("fsdp", None),
        P("rep", None, "fsdp"),
        P("rep", "fsdp", None),
        P("rep"),
        P("rep"),
        P(),
    )
    return jax.shard_map(
        local,
        mesh=mesh,
        in_specs=placed,
        out_specs=(
            P("rep", "fsdp", None),
            P("rep", "fsdp", None),
            P("rep", None, "fsdp"),
            P("rep", "fsdp", None),
        ),
        check_vma=False,
    )
```

```python
import functools

import jax
import jax.numpy as jnp
import numpy as np
from jax import lax
from jax.experimental import pallas as pl
from jax.experimental.pallas import tpu as pltpu
from jax.sharding import PartitionSpec as P

MESH = pl.DeviceIdType.MESH
bf16, f32 = jnp.bfloat16, jnp.float32

NR = 16
NF = 16
T = 256
RT = T // NR
D = 8192
V = 1024
DS = D // NF
HALF = DS // 2
QUARTER = HALF // 2
A = 128
G = 4
GC = D // G

REPS = [(dz, dc) for dz in (4, 3, 5, 2, 6, 1, 7) for dc in (0, 1)] + [(0, 1)]
RING = (1, 3, 2)
FAR = T // 2


def nt(a, b):
    return lax.dot_general(a, b, (((1,), (1,)), ((), ())), preferred_element_type=f32)


def tn(a, b):
    return lax.dot_general(a, b, (((0,), (0,)), ((), ())), preferred_element_type=f32)


def nn(a, b):
    return jnp.dot(a, b, preferred_element_type=f32)


def split(v):
    hi = v.astype(bf16)
    return hi, (v - hi.astype(f32)).astype(bf16)


def arrival_group(dz, dc, c):
    behind = -dz % 8
    if behind in (2, 6):
        return 6 + c * 9 if behind == 2 else 7 + c * 7
    return {0: 0, 1: 2, 7: 4, 4: 8, 5: 10, 3: 12}[behind] + dc


def kernel(
    tok, cot, w, down, up, sel, selt, lab, q,
    tg, val, dg, ug,
    xs, xr, gs, gr, wf, dn, upr, labr, dpart, ra, rb, sa, sb, ra2, rb2, upart, urecv,
    cotp, hc, gcat, hg, gtcat, upb, acc, mid,
    tok_sem, x_send, x_recv, lab_sem, hop_sem, hop_own, up_sem, dn_send, dn_recv, w_own, w_send, w_recv,
    sib_send, sib_recv, far_sem, g_send, g_recv, r_sem, r2_sem, u_sem, out_sem,
):
    rep, fs = lax.axis_index("rep"), lax.axis_index("fsdp")
    z, c, x, y = rep // 2, rep % 2, fs // 4, fs % 4
    plane = [((x + dx) % 4) * 4 + (y + dy) % 4 for dx in range(4) for dy in range(4)][1:]
    reps = [((z + dz) % 8) * 2 + (c + dc) % 2 for dz, dc in REPS]
    sib = rep + 1 - 2 * c
    opposite = ((z + 4) % 8) * 2 + c
    at_x = [((x + d) % 4) * 4 + y for d in RING]
    at_y = [x * 4 + (y + d) % 4 for d in RING]

    barrier = pltpu.get_barrier_semaphore()
    for r in reps:
        pl.semaphore_signal(barrier, inc=1, device_id=(r, fs), device_id_type=MESH)
    for f in plane:
        pl.semaphore_signal(barrier, inc=1, device_id=(rep, f), device_id_type=MESH)

    def group(g):
        return pl.ds(pl.multiple_of(g * GC, GC), GC)

    def loads(g):
        return pltpu.make_async_copy(tok.at[:, group(g)], gs.at[:, group(g)], tok_sem.at[g])

    for g in range(G):
        loads(g).start()
    own_w = pltpu.make_async_copy(w, wf.at[pl.ds(pl.multiple_of(fs * DS, DS), DS)], w_own)
    own_w.start()
    own_down = pltpu.make_async_copy(down, dn.at[fs, :, pl.ds(0, 64), :], hop_own)
    own_down.start()
    mine8 = pl.ds(pl.multiple_of(fs * 8, 8), 8)
    pltpu.make_async_copy(up, upr.at[mine8], up_sem.at[1]).start()
    pl.semaphore_wait(barrier, len(reps) + len(plane))

    def rows(r):
        return pl.ds(pl.multiple_of(r * RT, RT), RT)

    def push(src, dst, send, recv, r, f):
        pltpu.make_async_remote_copy(
            src_ref=src, dst_ref=dst, send_sem=send, recv_sem=recv,
            device_id=(r, f), device_id_type=MESH,
        ).start()

    def done(ref, sem):
        pltpu.make_async_copy(ref, ref, sem).wait()

    for (dz, dc), r in zip(REPS, reps):
        push(lab.at[rows(r)], labr.at[rows(arrival_group(dz, dc, c))], lab_sem.at[0], lab_sem.at[1], r, fs)
    pltpu.make_async_copy(lab.at[rows(rep)], labr.at[pl.ds(0, RT)], lab_sem.at[1]).start()
    push(down, dn.at[fs, :, pl.ds(64, 64), :], hop_sem.at[0], hop_sem.at[1], opposite, fs)
    for f in plane:
        push(up, upr.at[mine8], up_sem.at[0], up_sem.at[1], rep, f)

    def wpart(f, h, core):
        return wf.at[pl.ds(pl.multiple_of(f * DS + core * HALF + h * QUARTER, QUARTER), QUARTER)]

    def push_w(f, h, to):
        push(wpart(f, h, c), wpart(f, h, c), w_send, w_recv.at[f, h], rep, to)

    def push_dn(f, h, to):
        push(dn.at[f, h], dn.at[f, h], dn_send, dn_recv.at[f, h], rep, to)

    own_w.wait()
    for k in range(3):
        push_w(fs, 0, at_x[k])
        push_w(fs, 1, at_y[k])
    for k in range(3):
        push_w(fs, 0, at_y[k])
        push_w(fs, 1, at_x[k])

    def tokens_off(g):
        loads(g).wait()
        for k in range(GC // 512):
            cols = pl.ds(g * GC + k * 512, 512)
            xs[:, cols] = nn(sel[...], gs[:, cols]).astype(bf16)
        for (dz, dc), r in zip(REPS, reps):
            push(
                xs.at[rows(r), group(g)], xr.at[rows(arrival_group(dz, dc, c)), group(g)],
                x_send.at[g], x_recv.at[g], r, fs,
            )
        pltpu.make_async_copy(
            xs.at[rows(rep), group(g)], xr.at[pl.ds(0, RT), group(g)], x_recv.at[g]
        ).start()

    tokens_off(0)

    done(labr, lab_sem.at[1])
    cotp[...] = nn(labr[:, :T], cot[...]).astype(bf16)
    done(upr, up_sem.at[1])
    upb[...] = nn(q[...], upr[...].astype(bf16)).astype(bf16)
    lane = lax.broadcasted_iota(jnp.int32, (T, 2 * A), 1)
    row = lax.broadcasted_iota(jnp.int32, (T, 2 * A), 0)
    second = (lane % A) >= 64
    mask = labr[:, T:].astype(f32)
    back = jnp.where(second == (row >= FAR), 2.0 * nt(cotp[...], upb[...]) * mask, 0.0)
    hi, lo = split(back)
    gcat[:, : 2 * A] = hi
    gcat[:, 2 * A :] = lo
    far = pl.ds(FAR, FAR)
    push(cotp.at[far], hc.at[far], far_sem.at[0], far_sem.at[1], opposite, fs)
    push(gcat.at[far], hg.at[far], far_sem.at[2], far_sem.at[3], opposite, fs)
    hc[:FAR, :] = cotp[:FAR, :]
    hg[:FAR, :] = gcat[:FAR, :]
    own_down.wait()
    done(dn.at[0, :, pl.ds(0, 64), :], hop_sem.at[1])
    for k in range(3):
        push_dn(fs, 0, at_x[k])
        push_dn(fs, 1, at_y[k])
    for k in range(3):
        push_dn(fs, 0, at_y[k])
        push_dn(fs, 1, at_x[k])
    backt = back.T
    folded = jnp.concatenate(
        [backt[0:64] + backt[64:128], backt[128:192] + backt[192:256]], axis=0
    )
    hi, lo = split(folded)
    gtcat[:A, :] = hi
    gtcat[A:, :] = lo

    tokens_off(1)

    for k in range(3):
        fx, fy = ((x + 4 - RING[k]) % 4) * 4 + y, x * 4 + (y + 4 - RING[k]) % 4
        done(wpart(fx, 0, c), w_recv.at[fx, 0])
        done(wpart(fy, 1, c), w_recv.at[fy, 1])
        for j in range(3):
            push_w(fx, 0, at_y[j])
            push_w(fy, 1, at_x[j])
    tokens_off(2)
    for k in range(3):
        fx, fy = ((x + 4 - RING[k]) % 4) * 4 + y, x * 4 + (y + 4 - RING[k]) % 4
        done(dn.at[fx, 0], dn_recv.at[fx, 0])
        done(dn.at[fy, 1], dn_recv.at[fy, 1])
        for j in range(3):
            push_dn(fx, 0, at_y[j])
            push_dn(fy, 1, at_x[j])
    tokens_off(3)
    done(hc.at[far], far_sem.at[1])
    done(hg.at[far], far_sem.at[3])

    def dcols(f):
        return pl.ds(pl.multiple_of(f * DS, DS), DS)

    owner, other = rep, opposite
    back_to = []
    for dz, base in ((0, 0), (1, 2), (7, 4)):
        for dc in (0, 1):
            back_to.append((base + dc, ((z + dz) % 8) * 2 + (c + dc) % 2, owner))
            back_to.append((8 + base + dc, ((z + dz) % 8) * 2 + (c + dc) % 2, other))
    for k, dz in ((6, 2), (7, 6)):
        back_to.append((k, ((z + dz) % 8) * 2, owner))
        back_to.append((8 + k, ((z + dz) % 8) * 2 + 1, other))
    remote = [e for e in back_to if e[0] not in (0, 8)]
    remote = remote[-4:] + remote[:-4]

    def grads(f):
        dv = dn[f].reshape(2 * A, DS)
        out = nt(hc[...], wf[dcols(f), :])
        out = out + nn(hg[:, : 2 * A], dv) + nn(hg[:, 2 * A :], dv)
        gs[:, dcols(f)] = out.astype(bf16)
        for k, r, place in remote:
            push(
                gs.at[pl.ds(k * RT, RT), dcols(f)], gr.at[rows(place), dcols(f)],
                g_send.at[f], g_recv.at[f], r, fs,
            )
        for k, place in ((0, owner), (8, other)):
            pltpu.make_async_copy(
                gs.at[pl.ds(k * RT, RT), dcols(f)], gr.at[rows(place), dcols(f)], g_recv.at[f]
            ).start()

    grads(fs)

    def from_offset(i):
        return ((x + 4 - i % 4) % 4) * 4 + (y + 4 - i // 4) % 4

    def whalf(f, core):
        return wf.at[pl.ds(pl.multiple_of(f * DS + core * HALF, HALF), HALF)]

    def half_in(i):
        f = from_offset(i)
        @pl.when(i // 4 != 0)
        def _():
            done(wpart(f, 0, c), w_recv.at[f, 0])
            done(dn.at[f, 0], dn_recv.at[f, 0])

        @pl.when(i % 4 != 0)
        def _():
            done(wpart(f, 1, c), w_recv.at[f, 1])
            done(dn.at[f, 1], dn_recv.at[f, 1])

        push(whalf(f, c), whalf(f, c), sib_send, sib_recv.at[f], sib, fs)

    half_in(1)

    def step(i, _):
        @pl.when(i < 15)
        def _():
            half_in(i + 1)

        f = from_offset(i)
        done(whalf(f, 1 - c), sib_recv.at[f])
        grads(f)
        return 0

    lax.fori_loop(1, 16, step, 0)

    acc[...] = jnp.zeros_like(acc)
    mid[...] = jnp.zeros_like(mid)

    def fwd_group(g, _):
        done(xr.at[:, group(g)], x_recv.at[g])

        def fwd(k, _):
            fy = (y + k) % 4
            f = g * 4 + fy
            xv = xr[:, dcols(f)]
            part = nn(gtcat[...], xv)
            dpart[f] = part[:A] + part[A:]

            @pl.when(g != x)
            def _():
                push(dpart.at[f, pl.ds(0, 64)], ra.at[x, fy], r_sem.at[0], r_sem.at[1], rep, g * 4 + y)

            @pl.when(fy != y)
            def _():
                push(dpart.at[f, pl.ds(64, 64)], rb.at[y, g], r_sem.at[2], r_sem.at[3], rep, x * 4 + fy)

            acc[...] += nn(xv, wf[dcols(f), :])
            mid[...] += nt(xv, dn[f].reshape(2 * A, DS))
            return 0

        lax.fori_loop(0, 4, fwd, 0)
        return 0

    lax.fori_loop(0, G, fwd_group, 0)

    m2 = jnp.where(second, 0.0, 2.0 * mid[...] * mask)
    hi, lo = split(m2)
    out = acc[...] + nn(hi, upb[...]) + nn(lo, upb[...])
    val[...] = tn(labr[:, :T], out.astype(bf16)).astype(bf16)
    hi, lo = split(m2.T)
    hi = tn(q[...], hi).astype(bf16)
    lo = tn(q[...], lo).astype(bf16)
    upart[...] = nn(hi, cotp[...]) + nn(lo, cotp[...])
    for f in plane:
        push(upart.at[pl.ds(pl.multiple_of(f * 8, 8), 8)], urecv.at[fs], u_sem.at[0], u_sem.at[1], rep, f)
    pltpu.make_async_copy(upart.at[mine8], urecv.at[fs], u_sem.at[1]).start()

    done(ra.at[pl.ds(0, 3)], r_sem.at[1])
    done(rb.at[pl.ds(0, 3)], r_sem.at[3])

    def first_sum(k, _):
        own_a, own_b = dpart[x * 4 + k, :64, :], dpart[k * 4 + y, 64:, :]
        for d in RING:
            own_a = own_a + ra[(x + d) % 4, k]
            own_b = own_b + rb[(y + d) % 4, k]
        sa[k] = own_a
        sb[k] = own_b

        @pl.when(k != y)
        def _():
            push(sa.at[k], ra2.at[y], r2_sem.at[0], r2_sem.at[1], rep, x * 4 + k)

        @pl.when(k != x)
        def _():
            push(sb.at[k], rb2.at[x], r2_sem.at[2], r2_sem.at[3], rep, k * 4 + y)

        return 0

    lax.fori_loop(0, 4, first_sum, 0)

    for g in range(G):
        done(xs.at[pl.ds(0, T - RT), group(g)], x_send.at[g])

    def finish(i, _):
        f = from_offset(i)
        done(gr.at[:, dcols(f)], g_recv.at[f])
        xs[:, dcols(f)] = nn(selt[...], gr[:, dcols(f)]).astype(bf16)
        pltpu.make_async_copy(xs.at[:, dcols(f)], tg.at[:, dcols(f)], out_sem).start()
        return 0

    lax.fori_loop(0, 16, finish, 0)

    done(urecv, u_sem.at[1])
    ug[...] = jnp.sum(urecv[...], axis=0)
    done(ra2.at[pl.ds(0, 3)], r2_sem.at[1])
    done(rb2.at[pl.ds(0, 3)], r2_sem.at[3])
    sum_a, sum_b = sa[y], sb[x]
    for d in RING:
        sum_a = sum_a + ra2[(y + d) % 4]
        sum_b = sum_b + rb2[(x + d) % 4]
    dg[:64, :] = sum_a
    dg[64:, :] = sum_b

    done(tg, out_sem)
    done(lab.at[pl.ds(0, T - RT)], lab_sem.at[0])
    done(down, hop_sem.at[0])
    done(cotp.at[far], far_sem.at[0])
    done(gcat.at[far], far_sem.at[2])
    done(upr.at[pl.ds(0, 15 * 8)], up_sem.at[0])
    done(dn.at[pl.ds(0, 15)], dn_send)
    done(wf.at[pl.ds(0, 30 * QUARTER)], w_send)
    done(wf.at[pl.ds(0, 15 * HALF)], sib_send)
    done(ra.at[pl.ds(0, 3)], r_sem.at[0])
    done(rb.at[pl.ds(0, 3)], r_sem.at[2])
    done(ra2.at[pl.ds(0, 3)], r2_sem.at[0])
    done(rb2.at[pl.ds(0, 3)], r2_sem.at[2])
    done(upart.at[pl.ds(0, 15 * 8)], u_sem.at[0])

    def sent(f, _):
        done(gs.at[pl.ds(0, 14 * RT), dcols(f)], g_send.at[f])
        return 0

    lax.fori_loop(0, 16, sent, 0)


def rank_order():
    order = np.zeros((2 * A, A), np.float32)
    for k in range(2 * A):
        a, r = k // A, k % 64
        order[k, (r // 4) * 8 + a * 4 + r % 4] = 1.0
    return order


def local(
    tokens,
    cotangent,
    frozen_weight,
    down_factor_table,
    up_factor_table,
    adapter_of_block,
    block_destination,
    adapter_table_row,
):
    blocks = tokens.shape[0]
    steps = jnp.arange(blocks, dtype=jnp.int32)
    wide = jnp.arange(T, dtype=jnp.int32)
    dest_rep = block_destination // blocks
    slot = block_destination % blocks
    row = jnp.sum(
        jnp.where(adapter_of_block[:, None] == steps[None, :], adapter_table_row[None, :], 0), axis=1
    )
    adapter = row - dest_rep * 2
    before = (dest_rep[:, None] == dest_rep[None, :]) & (steps[None, :] < steps[:, None])
    place = dest_rep * 2 + jnp.sum(before.astype(jnp.int32), axis=1)
    hit = place[None, :] == steps[:, None]
    slot_at = jnp.sum(jnp.where(hit, slot[None, :], 0), axis=1)
    adapter_at = jnp.sum(jnp.where(hit, adapter[None, :], 0), axis=1)

    def by_token(v):
        return jnp.broadcast_to(v[:, None], (blocks, 8)).reshape(T)

    code = by_token(place) * 8 + wide % 8
    slot_code = by_token(slot_at) * 8 + wide % 8
    sel = (wide[:, None] == code[None, :]).astype(bf16)
    selt = (code[:, None] == wide[None, :]).astype(bf16)
    lab = jnp.concatenate(
        [
            (slot_code[:, None] == wide[None, :]).astype(bf16),
            (by_token(adapter_at)[:, None] == (wide // A)[None, :]).astype(bf16),
        ],
        axis=1,
    )
    q = jnp.asarray(rank_order(), bf16)

    vm = pl.BlockSpec(memory_space=pltpu.VMEM)
    hbm = pl.BlockSpec(memory_space=pl.ANY)
    dma = pltpu.SemaphoreType.DMA
    tg, val, dg, ug = pl.pallas_call(
        kernel,
        out_shape=(
            jax.ShapeDtypeStruct((T, D), bf16),
            jax.ShapeDtypeStruct((T, V), bf16),
            jax.ShapeDtypeStruct((A, DS), f32),
            jax.ShapeDtypeStruct((8, V), f32),
        ),
        in_specs=[hbm, vm, hbm, hbm, hbm, vm, vm, vm, vm],
        out_specs=(hbm, vm, vm, vm),
        scratch_shapes=[
            pltpu.VMEM((T, D), bf16),
            pltpu.VMEM((T, D), bf16),
            pltpu.VMEM((T, D), bf16),
            pltpu.VMEM((T, D), bf16),
            pltpu.VMEM((D, V), bf16),
            pltpu.VMEM((NF, 2, A, DS), bf16),
            pltpu.VMEM((A, V), f32),
            pltpu.VMEM((T, 2 * T), bf16),
            pltpu.VMEM((NF, A, DS), f32),
            pltpu.VMEM((4, 4, 64, DS), f32),
            pltpu.VMEM((4, 4, 64, DS), f32),
            pltpu.VMEM((4, 64, DS), f32),
            pltpu.VMEM((4, 64, DS), f32),
            pltpu.VMEM((4, 64, DS), f32),
            pltpu.VMEM((4, 64, DS), f32),
            pltpu.VMEM((A, V), f32),
            pltpu.VMEM((NF, 8, V), f32),
            pltpu.VMEM((T, V), bf16),
            pltpu.VMEM((T, V), bf16),
            pltpu.VMEM((T, 4 * A), bf16),
            pltpu.VMEM((T, 4 * A), bf16),
            pltpu.VMEM((2 * A, T), bf16),
            pltpu.VMEM((2 * A, V), bf16),
            pltpu.VMEM((T, V), f32),
            pltpu.VMEM((T, 2 * A), f32),
            dma((G,)),
            dma((G,)),
            dma((G,)),
            dma((2,)),
            dma((2,)),
            dma,
            dma((2,)),
            dma,
            dma((NF, 2)),
            dma,
            dma,
            dma((NF, 2)),
            dma,
            dma((NF,)),
            dma((4,)),
            dma((NF,)),
            dma((NF,)),
            dma((4,)),
            dma((4,)),
            dma((2,)),
            dma,
        ],
        compiler_params=pltpu.CompilerParams(
            collective_id=0, has_side_effects=True, vmem_limit_bytes=60 * 1024 * 1024
        ),
        cost_estimate=pl.CostEstimate(
            flops=14 * 10**9, bytes_accessed=12 * 2**20, transcendentals=0
        ),
        name="lora_moves",
    )(
        tokens.reshape(T, D),
        cotangent.reshape(T, V),
        frozen_weight,
        down_factor_table,
        up_factor_table.astype(f32).reshape(8, V),
        sel,
        selt,
        lab,
        q,
    )
    return (
        val.reshape(blocks, 8, V),
        tg.reshape(blocks, 8, D),
        dg.reshape(2, 64, DS),
        ug.reshape(2, 4, V),
    )


def solution(mesh):
    placed = (
        P("rep", "fsdp", None),
        P("rep", "fsdp", None),
        P("fsdp", None),
        P("rep", None, "fsdp"),
        P("rep", "fsdp", None),
        P("rep"),
        P("rep"),
        P(),
    )
    return jax.shard_map(
        local,
        mesh=mesh,
        in_specs=placed,
        out_specs=(
            P("rep", "fsdp", None),
            P("rep", "fsdp", None),
            P("rep", None, "fsdp"),
            P("rep", "fsdp", None),
        ),
        check_vma=False,
    )
```

```python
import functools

import jax
import jax.numpy as jnp
import numpy as np
from jax import lax
from jax.experimental import pallas as pl
from jax.experimental.pallas import tpu as pltpu
from jax.sharding import PartitionSpec as P

MESH = pl.DeviceIdType.MESH
bf16, f32 = jnp.bfloat16, jnp.float32

NR = 16
NF = 16
T = 256
RT = T // NR
D = 8192
V = 1024
DS = D // NF
HALF = DS // 2
QUARTER = HALF // 2
A = 128
G = 4
GC = D // G

REPS = [(dz, dc) for dz in (4, 3, 5, 2, 6, 1, 7) for dc in (0, 1)] + [(0, 1)]
RING = (1, 3, 2)
STEPS = (
    (),
    (
        ((1, 0), ((1, 0), (0, 1), (0, -1))),
        ((3, 0), ((0, 1), (0, -1))),
        ((0, 1), ((0, 1),)),
    ),
    (
        ((2, 0), ((0, 1), (0, -1))),
        ((1, 3), ((0, -1),)),
        ((3, 3), ((0, -1),)),
    ),
    (((2, 1), ((0, 1),)),),
)
PASSED = frozenset(off for step in STEPS for off, _ in step)
FAR = T // 2


def nt(a, b):
    return lax.dot_general(a, b, (((1,), (1,)), ((), ())), preferred_element_type=f32)


def tn(a, b):
    return lax.dot_general(a, b, (((0,), (0,)), ((), ())), preferred_element_type=f32)


def nn(a, b):
    return jnp.dot(a, b, preferred_element_type=f32)


def split(v):
    hi = v.astype(bf16)
    return hi, (v - hi.astype(f32)).astype(bf16)


ORDER = {0: 0, 1: 1, 7: 2, 6: 3, 3: 4, 4: 5, 2: 6, 5: 7}
NEAR = (0, 1, -1, -2)
OTHER = (0, 1, -1, 2)


def arrival_group(dz, dc, c):
    to = (c + dc) % 2
    up, low = ORDER[-dz % 8], ORDER[dz % 8]
    return 2 * (up + to * (low - up)) + dc


def kernel(
    tok, cot, w, down, up, sel, selt, lab, q,
    tg, val, dg, ug,
    xs, xr, gs, gr, wf, dn, ups, upc, upr, labr, dpart, ra, rb, sa, sb, ra2, rb2, upart, urecv,
    cotp, hc, hg, gtcat, upb, acc, mid,
    tok_sem, x_send, x_recv, lab_sem, hop_sem, hop_own, up_sem, dn_send, dn_recv, w_own, w_send, w_recv,
    sib_send, sib_recv, far_sem, g_send, g_recv, r_sem, r2_sem, u_sem, out_sem,
):
    rep, fs = lax.axis_index("rep"), lax.axis_index("fsdp")
    z, c, x, y = rep // 2, rep % 2, fs // 4, fs % 4
    plane = [((x + dx) % 4) * 4 + (y + dy) % 4 for dx in range(4) for dy in range(4)][1:]
    reps = [((z + dz) % 8) * 2 + (c + dc) % 2 for dz, dc in REPS]
    sib = rep + 1 - 2 * c
    turn = 3 - 6 * c
    opposite = ((z + turn + 8) % 8) * 2 + c
    partner = ((z - turn + 8) % 8) * 2 + c

    barrier = pltpu.get_barrier_semaphore()
    for r in reps:
        pl.semaphore_signal(barrier, inc=1, device_id=(r, fs), device_id_type=MESH)
    for f in plane:
        pl.semaphore_signal(barrier, inc=1, device_id=(rep, f), device_id_type=MESH)

    def group(g):
        return pl.ds(pl.multiple_of(g * GC, GC), GC)

    def loads(g):
        return pltpu.make_async_copy(tok.at[:, group(g)], gs.at[:, group(g)], tok_sem.at[g])

    for g in range(G):
        loads(g).start()
    own_w = pltpu.make_async_copy(w, wf.at[pl.ds(pl.multiple_of(fs * DS, DS), DS)], w_own)
    own_w.start()
    own_down = pltpu.make_async_copy(down, dn.at[fs, :, pl.ds(0, 64), :], hop_own)
    own_down.start()
    for a in range(2):
        ups[4 * a : 4 * a + 4, :] = up[a].astype(f32)

    for g in range(G):
        loads(g).wait()
        xs[:, group(g)] = nn(sel[...], gs[:, group(g)]).astype(bf16)
    pl.semaphore_wait(barrier, len(reps) + len(plane))

    def rows(r):
        return pl.ds(pl.multiple_of(r * RT, RT), RT)

    def push(src, dst, send, recv, r, f):
        pltpu.make_async_remote_copy(
            src_ref=src, dst_ref=dst, send_sem=send, recv_sem=recv,
            device_id=(r, f), device_id_type=MESH,
        ).start()

    def done(ref, sem):
        pltpu.make_async_copy(ref, ref, sem).wait()

    for (dz, dc), r in zip(REPS, reps):
        push(lab.at[rows(r)], labr.at[rows(arrival_group(dz, dc, c))], lab_sem.at[0], lab_sem.at[1], r, fs)
    pltpu.make_async_copy(lab.at[rows(rep)], labr.at[pl.ds(0, RT)], lab_sem.at[1]).start()
    push(ups.at[pl.ds(0, 8)], ups.at[pl.ds(8, 8)], up_sem.at[2], up_sem.at[3], opposite, fs)
    push(down, dn.at[fs, :, pl.ds(64, 64), :], hop_sem.at[0], hop_sem.at[1], opposite, fs)

    def wpart(f, h, core):
        return wf.at[pl.ds(pl.multiple_of(f * DS + core * HALF + h * QUARTER, QUARTER), QUARTER)]

    def push_w(f, h, to):
        push(wpart(f, h, c), wpart(f, h, c), w_send, w_recv.at[f, h], rep, to)

    def push_dn(f, h, to):
        push(dn.at[f, h], dn.at[f, h], dn_send, dn_recv.at[f, h], rep, to)

    def at(dx, dy):
        return ((x + dx + 4) % 4) * 4 + (y + dy + 4) % 4

    def source(off):
        return at(-off[0], -off[1])

    def ring(own_or, send):
        if own_or == 0:
            for d in (1, -1):
                send(source((0, 0)), 0, at(d, 0))
                send(source((0, 0)), 1, at(0, d))
            for d in (1, -1):
                send(source((0, 0)), 0, at(0, d))
                send(source((0, 0)), 1, at(d, 0))
        for off, goes in STEPS[own_or]:
            for h in (0, 1):
                o = off if h == 0 else off[::-1]
                ref, sem = unit(send, source(o), h)
                done(ref, sem)
                for to in goes:
                    t = to if h == 0 else to[::-1]
                    send(source(o), h, at(*t))

    def unit(send, f, h):
        if send is push_w:
            return wpart(f, h, c), w_recv.at[f, h]
        return dn.at[f, h], dn_recv.at[f, h]

    own_w.wait()
    ring(0, push_w)

    def tokens_off(g):
        for (dz, dc), r in zip(REPS, reps):
            push(
                xs.at[rows(r), group(g)], xr.at[rows(arrival_group(dz, dc, c)), group(g)],
                x_send.at[g], x_recv.at[g], r, fs,
            )
        pltpu.make_async_copy(
            xs.at[rows(rep), group(g)], xr.at[pl.ds(0, RT), group(g)], x_recv.at[g]
        ).start()

    tokens_off(0)

    done(labr, lab_sem.at[1])
    cotp[:, :V] = nn(labr[:, :T], cot[...]).astype(bf16)
    cotp[:, V:] = labr[:, T:]
    far = pl.ds(FAR, FAR)
    push(cotp.at[far], hc.at[far], far_sem.at[0], far_sem.at[1], opposite, fs)
    hc[:FAR, :] = cotp[:FAR, :]
    tokens_off(1)

    done(ups.at[pl.ds(0, 8)], up_sem.at[3])
    upc[...] = ups[...].astype(bf16)
    mine16 = pl.ds(pl.multiple_of(fs * 16, 16), 16)
    for f in plane:
        push(upc, upr.at[mine16], up_sem.at[0], up_sem.at[1], rep, f)
    upr[mine16, :] = upc[...]
    own_down.wait()
    done(dn.at[0, :, pl.ds(0, 64), :], hop_sem.at[1])
    ring(0, push_dn)
    tokens_off(2)
    tokens_off(3)

    done(upr.at[pl.ds(0, 15 * 16)], up_sem.at[1])
    upb[...] = nn(q[...], upr[...]).astype(bf16)
    lane = lax.broadcasted_iota(jnp.int32, (T, 2 * A), 1)
    row = lax.broadcasted_iota(jnp.int32, (T, 2 * A), 0)
    second = (lane % A) >= 64

    def chosen(ref):
        ids = ref[:, V:].astype(f32)
        return jnp.concatenate([1.0 - ids, ids], axis=1)

    mask = jnp.where(second, 0.0, chosen(cotp))
    backt = (2.0 * nt(cotp[:, :V], upb[...]) * mask).T
    hi, lo = split(jnp.concatenate([backt[0:64], backt[128:192]], axis=0))
    gtcat[:A, :] = hi
    gtcat[A:, :] = lo
    done(hc.at[far], far_sem.at[1])
    back = jnp.where(second == (row >= FAR), 2.0 * nt(hc[:, :V], upb[...]) * chosen(hc), 0.0)
    hi, lo = split(back)
    hg[:, : 2 * A] = hi
    hg[:, 2 * A :] = lo

    def dcols(f):
        return pl.ds(pl.multiple_of(f * DS, DS), DS)

    owner, other = rep, partner
    back_to = []
    for k in range(4):
        for dc in (0, 1):
            core = (c + dc) % 2
            way = 1 - 2 * c
            back_to.append((2 * k + dc, ((z + way * NEAR[k] + 8) % 8) * 2 + core, owner))
            back_to.append((8 + 2 * k + dc, ((z + way * OTHER[k] + 8) % 8) * 2 + core, other))
    remote = [e for e in back_to if e[0] not in (0, 8)]
    remote = remote[::-1]

    def grads(f):
        dv = dn[f].reshape(2 * A, DS)
        out = nt(hc[:, :V], wf[dcols(f), :])
        out = out + nn(hg[:, : 2 * A], dv) + nn(hg[:, 2 * A :], dv)
        gs[:, dcols(f)] = out.astype(bf16)

    def grads_off(g):
        for k, r, place in remote:
            push(
                gs.at[pl.ds(k * RT, RT), group(g)], gr.at[rows(place), group(g)],
                g_send.at[g], g_recv.at[g], r, fs,
            )
        for k, place in ((0, owner), (8, other)):
            pltpu.make_async_copy(
                gs.at[pl.ds(k * RT, RT), group(g)], gr.at[rows(place), group(g)], g_recv.at[g]
            ).start()

    def whalf(f, core):
        return wf.at[pl.ds(pl.multiple_of(f * DS + core * HALF, HALF), HALF)]

    def take_in(offs):
        for off in offs:
            f = source(off)
            for h in (0, 1):
                if (off if h == 0 else off[::-1]) not in PASSED:
                    done(wpart(f, h, c), w_recv.at[f, h])
                    done(dn.at[f, h], dn_recv.at[f, h])
            push(whalf(f, c), whalf(f, c), sib_send, sib_recv.at[f], sib, fs)

    def grads_of(count, dx, dy):
        def step(i, _):
            f = ((x + 4 - dx(i)) % 4) * 4 + (y + 4 - dy(i)) % 4
            done(whalf(f, 1 - c), sib_recv.at[f])
            grads(f)
            return 0

        lax.fori_loop(0, count, step, 0)

    def down_terms(g):
        def term(k, _):
            fy = (y + k) % 4
            f = g * 4 + fy
            part = nn(gtcat[...], xr[:, dcols(f)])
            dpart[f] = part[:A] + part[A:]

            @pl.when(g != x)
            def _():
                push(dpart.at[f, pl.ds(0, 64)], ra.at[x, fy], r_sem.at[0], r_sem.at[1], rep, g * 4 + y)

            @pl.when(fy != y)
            def _():
                push(dpart.at[f, pl.ds(64, 64)], rb.at[y, g], r_sem.at[2], r_sem.at[3], rep, x * 4 + fy)

            return 0

        lax.fori_loop(0, 4, term, 0)

    def odd(i):
        return 1 + 2 * (i % 2)

    ring(1, push_w)
    ring(1, push_dn)
    take_in([(1, 0), (3, 0), (0, 1), (0, 3)])
    grads(fs)
    grads_of(4, lambda i: odd(i) * (1 - i // 2), lambda i: odd(i) * (i // 2))
    ring(2, push_w)
    ring(2, push_dn)
    take_in([(2, 0), (0, 2), (1, 1), (3, 1), (1, 3), (3, 3)])
    grads_of(2, lambda i: 2 - 2 * i, lambda i: 2 * i)
    ring(3, push_w)
    ring(3, push_dn)
    grads_of(4, lambda i: odd(i), lambda i: 1 + 2 * (i // 2))
    take_in([(2, 1), (2, 3), (1, 2), (3, 2), (2, 2)])
    grads_of(4, lambda i: 2 - (1 - 2 * (i % 2)) * (i // 2), lambda i: odd(i) + (2 - odd(i)) * (i // 2))
    grads_of(1, lambda i: 2, lambda i: 2)

    def arrived(g, _):
        done(xr.at[:, group(g)], x_recv.at[g])
        grads_off(g)
        down_terms(g)
        return 0

    lax.fori_loop(0, G, arrived, 0)

    acc[...] = jnp.zeros_like(acc)
    mid[...] = jnp.zeros_like(mid)

    def fwd(g, _):
        acc[...] += nn(xr[:, group(g)], wf[group(g), :])
        return 0

    def low(f, _):
        mid[...] += nt(xr[:, dcols(f)], dn[f].reshape(2 * A, DS))
        return 0

    lax.fori_loop(0, G, fwd, 0)
    lax.fori_loop(0, NF, low, 0)

    m2 = 2.0 * mid[...] * mask
    hi, lo = split(m2)
    out = acc[...] + nn(hi, upb[...]) + nn(lo, upb[...])
    val[...] = tn(labr[:, :T], out.astype(bf16)).astype(bf16)
    hi, lo = split(m2.T)
    hi = tn(q[...], hi).astype(bf16)
    lo = tn(q[...], lo).astype(bf16)
    own_cot = cotp[:, :V]
    upart[...] = nn(hi, own_cot) + nn(lo, own_cot)
    for f in plane:
        push(upart.at[pl.ds(pl.multiple_of(f * 16, 16), 8)], urecv.at[fs], u_sem.at[0], u_sem.at[1], rep, f)
    mine8 = pl.ds(pl.multiple_of(fs * 16, 16), 8)
    pltpu.make_async_copy(upart.at[mine8], urecv.at[fs], u_sem.at[1]).start()

    done(ra.at[pl.ds(0, 3)], r_sem.at[1])
    done(rb.at[pl.ds(0, 3)], r_sem.at[3])

    def first_sum(k, _):
        own_a, own_b = dpart[x * 4 + k, :64, :], dpart[k * 4 + y, 64:, :]
        for d in RING:
            own_a = own_a + ra[(x + d) % 4, k]
            own_b = own_b + rb[(y + d) % 4, k]
        sa[k] = own_a
        sb[k] = own_b

        @pl.when(k != y)
        def _():
            push(sa.at[k], ra2.at[y], r2_sem.at[0], r2_sem.at[1], rep, x * 4 + k)

        @pl.when(k != x)
        def _():
            push(sb.at[k], rb2.at[x], r2_sem.at[2], r2_sem.at[3], rep, k * 4 + y)

        return 0

    lax.fori_loop(0, 4, first_sum, 0)

    for g in range(G):
        done(xs.at[pl.ds(0, T - RT), group(g)], x_send.at[g])

    def finish(g, _):
        done(gr.at[:, group(g)], g_recv.at[g])
        xs[:, group(g)] = nn(selt[...], gr[:, group(g)]).astype(bf16)
        pltpu.make_async_copy(xs.at[:, group(g)], tg.at[:, group(g)], out_sem).start()
        return 0

    lax.fori_loop(0, G, finish, 0)

    done(urecv, u_sem.at[1])
    up_total = jnp.sum(urecv[...], axis=0)
    for a in range(2):
        ug[a] = up_total[4 * a : 4 * a + 4]
    done(ra2.at[pl.ds(0, 3)], r2_sem.at[1])
    done(rb2.at[pl.ds(0, 3)], r2_sem.at[3])
    sum_a, sum_b = sa[y], sb[x]
    for d in RING:
        sum_a = sum_a + ra2[(y + d) % 4]
        sum_b = sum_b + rb2[(x + d) % 4]
    dg[0] = sum_a
    dg[1] = sum_b

    done(tg, out_sem)
    done(lab.at[pl.ds(0, T - RT)], lab_sem.at[0])
    done(down, hop_sem.at[0])
    done(cotp.at[far], far_sem.at[0])
    done(upr.at[pl.ds(0, 15 * 16)], up_sem.at[0])
    done(ups.at[pl.ds(0, 8)], up_sem.at[2])
    done(dn.at[pl.ds(0, 15)], dn_send)
    done(wf.at[pl.ds(0, 30 * QUARTER)], w_send)
    done(wf.at[pl.ds(0, 15 * HALF)], sib_send)
    done(ra.at[pl.ds(0, 3)], r_sem.at[0])
    done(rb.at[pl.ds(0, 3)], r_sem.at[2])
    done(ra2.at[pl.ds(0, 3)], r2_sem.at[0])
    done(rb2.at[pl.ds(0, 3)], r2_sem.at[2])
    done(upart.at[pl.ds(0, 15 * 8)], u_sem.at[0])

    for g in range(G):
        done(gs.at[pl.ds(0, 14 * RT), group(g)], g_send.at[g])


def rank_order():
    order = np.zeros((2 * A, 2 * A), np.float32)
    for k in range(2 * A):
        a, d, r = k // A, k // 64 % 2, k % 64
        order[k, (r // 4) * 16 + d * 8 + a * 4 + r % 4] = 1.0
    return order


def local(
    tokens,
    cotangent,
    frozen_weight,
    down_factor_table,
    up_factor_table,
    adapter_of_block,
    block_destination,
    adapter_table_row,
):
    blocks = tokens.shape[0]
    steps = jnp.arange(blocks, dtype=jnp.int32)
    wide = jnp.arange(T, dtype=jnp.int32)
    dest_rep = block_destination // blocks
    slot = block_destination % blocks
    row = jnp.sum(
        jnp.where(adapter_of_block[:, None] == steps[None, :], adapter_table_row[None, :], 0), axis=1
    )
    adapter = row - dest_rep * 2
    before = (dest_rep[:, None] == dest_rep[None, :]) & (steps[None, :] < steps[:, None])
    place = dest_rep * 2 + jnp.sum(before.astype(jnp.int32), axis=1)
    hit = place[None, :] == steps[:, None]
    slot_at = jnp.sum(jnp.where(hit, slot[None, :], 0), axis=1)
    adapter_at = jnp.sum(jnp.where(hit, adapter[None, :], 0), axis=1)

    def by_token(v):
        return jnp.broadcast_to(v[:, None], (blocks, 8)).reshape(T)

    code = by_token(place) * 8 + wide % 8
    slot_code = by_token(slot_at) * 8 + wide % 8
    sel = (wide[:, None] == code[None, :]).astype(bf16)
    selt = (code[:, None] == wide[None, :]).astype(bf16)
    lab = jnp.concatenate(
        [
            (slot_code[:, None] == wide[None, :]).astype(bf16),
            jnp.broadcast_to(by_token(adapter_at)[:, None], (T, A)).astype(bf16),
        ],
        axis=1,
    )
    q = jnp.asarray(rank_order(), bf16)

    vm = pl.BlockSpec(memory_space=pltpu.VMEM)
    hbm = pl.BlockSpec(memory_space=pl.ANY)
    dma = pltpu.SemaphoreType.DMA
    tg, val, dg, ug = pl.pallas_call(
        kernel,
        out_shape=(
            jax.ShapeDtypeStruct((T, D), bf16),
            jax.ShapeDtypeStruct((T, V), bf16),
            jax.ShapeDtypeStruct((2, 64, DS), f32),
            jax.ShapeDtypeStruct((2, 4, V), f32),
        ),
        in_specs=[hbm, vm, hbm, hbm, vm, vm, vm, vm, vm],
        out_specs=(hbm, vm, vm, vm),
        scratch_shapes=[
            pltpu.VMEM((T, D), bf16),
            pltpu.VMEM((T, D), bf16),
            pltpu.VMEM((T, D), bf16),
            pltpu.VMEM((T, D), bf16),
            pltpu.VMEM((D, V), bf16),
            pltpu.VMEM((NF, 2, A, DS), bf16),
            pltpu.VMEM((16, V), f32),
            pltpu.VMEM((16, V), bf16),
            pltpu.VMEM((2 * A, V), bf16),
            pltpu.VMEM((T, T + A), bf16),
            pltpu.VMEM((NF, A, DS), f32),
            pltpu.VMEM((4, 4, 64, DS), f32),
            pltpu.VMEM((4, 4, 64, DS), f32),
            pltpu.VMEM((4, 64, DS), f32),
            pltpu.VMEM((4, 64, DS), f32),
            pltpu.VMEM((4, 64, DS), f32),
            pltpu.VMEM((4, 64, DS), f32),
            pltpu.VMEM((2 * A, V), f32),
            pltpu.VMEM((NF, 8, V), f32),
            pltpu.VMEM((T, V + A), bf16),
            pltpu.VMEM((T, V + A), bf16),
            pltpu.VMEM((T, 4 * A), bf16),
            pltpu.VMEM((2 * A, T), bf16),
            pltpu.VMEM((2 * A, V), bf16),
            pltpu.VMEM((T, V), f32),
            pltpu.VMEM((T, 2 * A), f32),
            dma((G,)),
            dma((G,)),
            dma((G,)),
            dma((2,)),
            dma((2,)),
            dma,
            dma((4,)),
            dma,
            dma((NF, 2)),
            dma,
            dma,
            dma((NF, 2)),
            dma,
            dma((NF,)),
            dma((2,)),
            dma((G,)),
            dma((G,)),
            dma((4,)),
            dma((4,)),
            dma((2,)),
            dma,
        ],
        compiler_params=pltpu.CompilerParams(
            collective_id=0, has_side_effects=True, vmem_limit_bytes=60 * 1024 * 1024
        ),
        cost_estimate=pl.CostEstimate(
            flops=14 * 10**9, bytes_accessed=12 * 2**20, transcendentals=0
        ),
        name="lora_moves",
    )(
        tokens.reshape(T, D),
        cotangent.reshape(T, V),
        frozen_weight,
        down_factor_table,
        up_factor_table,
        sel,
        selt,
        lab,
        q,
    )
    return (
        val.reshape(blocks, 8, V),
        tg.reshape(blocks, 8, D),
        dg,
        ug,
    )


def solution(mesh):
    placed = (
        P("rep", "fsdp", None),
        P("rep", "fsdp", None),
        P("fsdp", None),
        P("rep", None, "fsdp"),
        P("rep", "fsdp", None),
        P("rep"),
        P("rep"),
        P(),
    )
    return jax.shard_map(
        local,
        mesh=mesh,
        in_specs=placed,
        out_specs=(
            P("rep", "fsdp", None),
            P("rep", "fsdp", None),
            P("rep", None, "fsdp"),
            P("rep", "fsdp", None),
        ),
        check_vma=False,
    )
```

```python
import functools

import jax
import jax.numpy as jnp
import numpy as np
from jax import lax
from jax.experimental import pallas as pl
from jax.experimental.pallas import tpu as pltpu
from jax.sharding import PartitionSpec as P

MESH = pl.DeviceIdType.MESH
bf16, f32 = jnp.bfloat16, jnp.float32

NR = 16
NF = 16
T = 256
RT = T // NR
D = 8192
V = 1024
DS = D // NF
HALF = DS // 2
QUARTER = HALF // 2
A = 128
G = 4
GC = D // G

REPS = [(dz, dc) for dz in (4, 3, 5, 2, 6, 1, 7) for dc in (0, 1)] + [(0, 1)]
RING = (1, 3, 2)
STEPS = (
    (),
    (
        ((1, 0), ((1, 0), (0, 1), (0, -1))),
        ((3, 0), ((0, 1), (0, -1))),
        ((0, 1), ((0, 1),)),
    ),
    (
        ((2, 0), ((0, 1), (0, -1))),
        ((1, 3), ((0, -1),)),
        ((3, 3), ((0, -1),)),
    ),
    (((2, 1), ((0, 1),)),),
)
PASSED = frozenset(off for step in STEPS for off, _ in step)


def nt(a, b):
    return lax.dot_general(a, b, (((1,), (1,)), ((), ())), preferred_element_type=f32)


def tn(a, b):
    return lax.dot_general(a, b, (((0,), (0,)), ((), ())), preferred_element_type=f32)


def nn(a, b):
    return jnp.dot(a, b, preferred_element_type=f32)


def split(v):
    hi = v.astype(bf16)
    return hi, (v - hi.astype(f32)).astype(bf16)


ORDER = {0: 0, 1: 2, 7: 4, 3: 6, 2: 8, 5: 11, 6: 13}
OPPOSITE = (10, 15)
CUTS = (0, 96, 176, 256)
K3 = 192


def arrival_group(dz, dc, c):
    above = -dz % 8
    if above == 4:
        return OPPOSITE[0] + c * (OPPOSITE[1] - OPPOSITE[0])
    return ORDER[above] + dc


def kernel(
    tok, cot, w, down, up, sel, selt, lab, q, q8,
    tg, val, dg, ug,
    xs, xr, gs, gr, wf, dn, ups, upc, upr, labr, dpart, ra, rb, sa, sb, ra2, rb2, upart, urecv,
    cotp, hc, hg, gtcat, upb, acc, mid,
    tok_sem, x_send, x_recv, lab_sem, hop_sem, hop_own, up_sem, dn_send, dn_recv, w_own, w_send, w_recv,
    sib_send, sib_recv, far_sem, g_send, g_recv, r_sem, r2_sem, u_sem, out_sem,
):
    rep, fs = lax.axis_index("rep"), lax.axis_index("fsdp")
    z, c, x, y = rep // 2, rep % 2, fs // 4, fs % 4
    plane = [((x + dx) % 4) * 4 + (y + dy) % 4 for dx in range(4) for dy in range(4)][1:]
    reps = [((z + dz) % 8) * 2 + (c + dc) % 2 for dz, dc in REPS]
    sib = rep + 1 - 2 * c
    above, below = ((z + 3) % 8) * 2 + c, ((z + 5) % 8) * 2 + c

    barrier = pltpu.get_barrier_semaphore()
    for r in reps:
        pl.semaphore_signal(barrier, inc=1, device_id=(r, fs), device_id_type=MESH)
    for f in plane:
        pl.semaphore_signal(barrier, inc=1, device_id=(rep, f), device_id_type=MESH)

    def group(g):
        return pl.ds(pl.multiple_of(g * GC, GC), GC)

    def loads(g):
        return pltpu.make_async_copy(tok.at[:, group(g)], gs.at[:, group(g)], tok_sem.at[g])

    for g in range(G):
        loads(g).start()
    own_w = pltpu.make_async_copy(w, wf.at[pl.ds(pl.multiple_of(fs * DS, DS), DS)], w_own)
    own_w.start()
    own_down = pltpu.make_async_copy(down, dn.at[fs, :, pl.ds(0, 64), :], hop_own)
    own_down.start()
    for a in range(2):
        ups[4 * a : 4 * a + 4, :] = up[a].astype(f32)
    ups[24:, :] = jnp.zeros((8, V), f32)

    for g in range(G):
        loads(g).wait()
        xs[:, group(g)] = nn(sel[...], gs[:, group(g)]).astype(bf16)
    pl.semaphore_wait(barrier, len(reps) + len(plane))

    def rows(r):
        return pl.ds(pl.multiple_of(r * RT, RT), RT)

    def push(src, dst, send, recv, r, f):
        pltpu.make_async_remote_copy(
            src_ref=src, dst_ref=dst, send_sem=send, recv_sem=recv,
            device_id=(r, f), device_id_type=MESH,
        ).start()

    def done(ref, sem):
        pltpu.make_async_copy(ref, ref, sem).wait()

    for (dz, dc), r in zip(REPS, reps):
        push(lab.at[rows(r)], labr.at[rows(arrival_group(dz, dc, c))], lab_sem.at[0], lab_sem.at[1], r, fs)
    pltpu.make_async_copy(lab.at[rows(rep)], labr.at[pl.ds(0, RT)], lab_sem.at[1]).start()
    for k, r in ((1, above), (2, below)):
        push(ups.at[pl.ds(0, 8)], ups.at[pl.ds(8 * k, 8)], up_sem.at[2], up_sem.at[2 + k], r, fs)
        push(down, dn.at[fs, :, pl.ds(64 * k, 64), :], hop_sem.at[0], hop_sem.at[k], r, fs)

    def wpart(f, h, core):
        return wf.at[pl.ds(pl.multiple_of(f * DS + core * HALF + h * QUARTER, QUARTER), QUARTER)]

    def push_w(f, h, to):
        push(wpart(f, h, c), wpart(f, h, c), w_send, w_recv.at[f, h], rep, to)

    def push_dn(f, h, to):
        push(dn.at[f, h], dn.at[f, h], dn_send, dn_recv.at[f, h], rep, to)

    def at(dx, dy):
        return ((x + dx + 4) % 4) * 4 + (y + dy + 4) % 4

    def source(off):
        return at(-off[0], -off[1])

    def ring(own_or, send):
        if own_or == 0:
            for d in (1, -1):
                send(source((0, 0)), 0, at(d, 0))
                send(source((0, 0)), 1, at(0, d))
            for d in (1, -1):
                send(source((0, 0)), 0, at(0, d))
                send(source((0, 0)), 1, at(d, 0))
        for off, goes in STEPS[own_or]:
            for h in (0, 1):
                o = off if h == 0 else off[::-1]
                ref, sem = unit(send, source(o), h)
                done(ref, sem)
                for to in goes:
                    t = to if h == 0 else to[::-1]
                    send(source(o), h, at(*t))

    def unit(send, f, h):
        if send is push_w:
            return wpart(f, h, c), w_recv.at[f, h]
        return dn.at[f, h], dn_recv.at[f, h]

    own_w.wait()
    ring(0, push_w)

    def tokens_off(g):
        for (dz, dc), r in zip(REPS, reps):
            push(
                xs.at[rows(r), group(g)], xr.at[rows(arrival_group(dz, dc, c)), group(g)],
                x_send.at[g], x_recv.at[g], r, fs,
            )
        pltpu.make_async_copy(
            xs.at[rows(rep), group(g)], xr.at[pl.ds(0, RT), group(g)], x_recv.at[g]
        ).start()

    tokens_off(0)

    done(labr, lab_sem.at[1])
    cotp[:, :V] = nn(labr[:, :T], cot[...]).astype(bf16)
    cotp[:, V:] = labr[:, T:]
    served = [pl.ds(CUTS[k], CUTS[k + 1] - CUTS[k]) for k in range(3)]
    for k, r in ((1, above), (2, below)):
        push(cotp.at[served[k]], hc.at[served[k]], far_sem.at[0], far_sem.at[k], r, fs)
    hc[served[0], :] = cotp[served[0], :]
    tokens_off(1)

    done(ups.at[pl.ds(0, 8)], up_sem.at[3])
    done(ups.at[pl.ds(0, 8)], up_sem.at[4])
    upc[...] = ups[...].astype(bf16)
    mine32 = pl.ds(pl.multiple_of(fs * 32, 32), 32)
    for f in plane:
        push(upc, upr.at[mine32], up_sem.at[0], up_sem.at[1], rep, f)
    upr[mine32, :] = upc[...]
    own_down.wait()
    done(down, hop_sem.at[1])
    done(down, hop_sem.at[2])
    ring(0, push_dn)
    tokens_off(2)
    tokens_off(3)

    done(upr.at[pl.ds(0, 15 * 32)], up_sem.at[1])
    upb[...] = nn(q[...], upr[...]).astype(bf16)
    own_up = jnp.concatenate([upb[:64, :], upb[K3 : K3 + 64, :]], axis=0)
    ids = cotp[:, V:].astype(f32)
    mask = jnp.where(lax.broadcasted_iota(jnp.int32, (T, A), 1) < 64, 1.0 - ids, ids)
    hi, lo = split((2.0 * nt(cotp[:, :V], own_up) * mask).T)
    gtcat[:A, :] = hi
    gtcat[A:, :] = lo
    done(hc.at[served[1]], far_sem.at[1])
    done(hc.at[served[2]], far_sem.at[2])
    lane = lax.broadcasted_iota(jnp.int32, (T, 2 * K3), 1)
    row = lax.broadcasted_iota(jnp.int32, (T, 2 * K3), 0)
    owner_at = jnp.where(row >= CUTS[2], 2, jnp.where(row >= CUTS[1], 1, 0))
    ids = hc[:, V:].astype(f32)
    ids = jnp.concatenate([ids, ids, ids], axis=1)
    chosen = jnp.where(lane < K3, 1.0 - ids, ids)
    lane = jnp.where(lane < K3, lane, lane - K3)
    at_lane = jnp.where(lane >= 128, 2, jnp.where(lane >= 64, 1, 0))
    back = jnp.where(at_lane == owner_at, 2.0 * nt(hc[:, :V], upb[...]) * chosen, 0.0)
    hi, lo = split(back)
    hg[:, : 2 * K3] = hi
    hg[:, 2 * K3 :] = lo

    def dcols(f):
        return pl.ds(pl.multiple_of(f * DS, DS), DS)

    back_to = []
    for dc in (0, 1):
        core = (c + dc) % 2
        for k, dz, place in (
            (0, 0, rep), (2, 1, rep), (4, 7, rep), (6, 0, below), (8, 7, below), (11, 0, above), (13, 1, above),
        ):
            back_to.append((k + dc, ((z + dz) % 8) * 2 + core, place))
    back_to.append((OPPOSITE[0], ((z + 1) % 8) * 2, below))
    back_to.append((OPPOSITE[1], ((z + 7) % 8) * 2 + 1, above))
    remote = [e for e in back_to if e[0] not in (0, 6, 11)]
    remote = remote[::-1]

    def grads(f):
        dv = dn[f].reshape(2 * K3, DS)
        out = nt(hc[:, :V], wf[dcols(f), :])
        out = out + nn(hg[:, : 2 * K3], dv) + nn(hg[:, 2 * K3 :], dv)
        gs[:, dcols(f)] = out.astype(bf16)

    def grads_off(g):
        for k, r, place in remote:
            push(
                gs.at[pl.ds(k * RT, RT), group(g)], gr.at[rows(place), group(g)],
                g_send.at[g], g_recv.at[g], r, fs,
            )
        for k, place in ((0, rep), (6, below), (11, above)):
            pltpu.make_async_copy(
                gs.at[pl.ds(k * RT, RT), group(g)], gr.at[rows(place), group(g)], g_recv.at[g]
            ).start()

    def whalf(f, core):
        return wf.at[pl.ds(pl.multiple_of(f * DS + core * HALF, HALF), HALF)]

    def take_in(offs):
        for off in offs:
            f = source(off)
            for h in (0, 1):
                if (off if h == 0 else off[::-1]) not in PASSED:
                    done(wpart(f, h, c), w_recv.at[f, h])
                    done(dn.at[f, h], dn_recv.at[f, h])
            push(whalf(f, c), whalf(f, c), sib_send, sib_recv.at[f], sib, fs)

    def grads_of(count, dx, dy):
        def step(i, _):
            f = ((x + 4 - dx(i)) % 4) * 4 + (y + 4 - dy(i)) % 4
            done(whalf(f, 1 - c), sib_recv.at[f])
            grads(f)
            return 0

        lax.fori_loop(0, count, step, 0)

    def down_terms(g):
        def term(k, _):
            fy = (y + k) % 4
            f = g * 4 + fy
            part = nn(gtcat[...], xr[:, dcols(f)])
            dpart[f] = part[:A] + part[A:]

            @pl.when(g != x)
            def _():
                push(dpart.at[f, pl.ds(0, 64)], ra.at[x, fy], r_sem.at[0], r_sem.at[1], rep, g * 4 + y)

            @pl.when(fy != y)
            def _():
                push(dpart.at[f, pl.ds(64, 64)], rb.at[y, g], r_sem.at[2], r_sem.at[3], rep, x * 4 + fy)

            return 0

        lax.fori_loop(0, 4, term, 0)

    def odd(i):
        return 1 + 2 * (i % 2)

    ring(1, push_w)
    ring(1, push_dn)
    take_in([(1, 0), (3, 0), (0, 1), (0, 3)])
    grads(fs)
    grads_of(4, lambda i: odd(i) * (1 - i // 2), lambda i: odd(i) * (i // 2))
    ring(2, push_w)
    ring(2, push_dn)
    take_in([(2, 0), (0, 2), (1, 1), (3, 1), (1, 3), (3, 3)])
    grads_of(2, lambda i: 2 - 2 * i, lambda i: 2 * i)
    ring(3, push_w)
    ring(3, push_dn)
    grads_of(4, lambda i: odd(i), lambda i: 1 + 2 * (i // 2))
    take_in([(2, 1), (2, 3), (1, 2), (3, 2), (2, 2)])
    grads_of(4, lambda i: 2 - (1 - 2 * (i % 2)) * (i // 2), lambda i: odd(i) + (2 - odd(i)) * (i // 2))
    grads_of(1, lambda i: 2, lambda i: 2)

    def arrived(g, _):
        done(xr.at[:, group(g)], x_recv.at[g])

        @pl.when(g + 1 < G)
        def _():
            grads_off(g + 1)

        down_terms(g)
        return 0

    grads_off(0)
    lax.fori_loop(0, G, arrived, 0)

    acc[...] = jnp.zeros_like(acc)
    mid[...] = jnp.zeros_like(mid)

    def fwd(g, _):
        acc[...] += nn(xr[:, group(g)], wf[group(g), :])
        return 0

    def low(f, _):
        mid[...] += nt(xr[:, dcols(f)], dn[f, :, pl.ds(0, 64), :].reshape(A, DS))
        return 0

    lax.fori_loop(0, G, fwd, 0)
    lax.fori_loop(0, NF, low, 0)

    m2 = 2.0 * mid[...] * mask
    hi, lo = split(m2)
    out = acc[...] + nn(hi, own_up) + nn(lo, own_up)
    val[...] = tn(labr[:, :T], out.astype(bf16)).astype(bf16)
    hi, lo = split(m2.T)
    hi = tn(q8[...], hi).astype(bf16)
    lo = tn(q8[...], lo).astype(bf16)
    own_cot = cotp[:, :V]
    upart[...] = nn(hi, own_cot) + nn(lo, own_cot)
    for f in plane:
        push(upart.at[pl.ds(pl.multiple_of(f * 8, 8), 8)], urecv.at[fs], u_sem.at[0], u_sem.at[1], rep, f)
    mine8 = pl.ds(pl.multiple_of(fs * 8, 8), 8)
    pltpu.make_async_copy(upart.at[mine8], urecv.at[fs], u_sem.at[1]).start()

    done(ra.at[pl.ds(0, 3)], r_sem.at[1])
    done(rb.at[pl.ds(0, 3)], r_sem.at[3])

    def first_sum(k, _):
        own_a, own_b = dpart[x * 4 + k, :64, :], dpart[k * 4 + y, 64:, :]
        for d in RING:
            own_a = own_a + ra[(x + d) % 4, k]
            own_b = own_b + rb[(y + d) % 4, k]
        sa[k] = own_a
        sb[k] = own_b

        @pl.when(k != y)
        def _():
            push(sa.at[k], ra2.at[y], r2_sem.at[0], r2_sem.at[1], rep, x * 4 + k)

        @pl.when(k != x)
        def _():
            push(sb.at[k], rb2.at[x], r2_sem.at[2], r2_sem.at[3], rep, k * 4 + y)

        return 0

    lax.fori_loop(0, 4, first_sum, 0)

    for g in range(G):
        done(xs.at[pl.ds(0, T - RT), group(g)], x_send.at[g])

    def finish(g, _):
        done(gr.at[:, group(g)], g_recv.at[g])
        xs[:, group(g)] = nn(selt[...], gr[:, group(g)]).astype(bf16)
        pltpu.make_async_copy(xs.at[:, group(g)], tg.at[:, group(g)], out_sem).start()
        return 0

    lax.fori_loop(0, G, finish, 0)

    done(urecv, u_sem.at[1])
    up_total = jnp.sum(urecv[...], axis=0)
    for a in range(2):
        ug[a] = up_total[4 * a : 4 * a + 4]
    done(ra2.at[pl.ds(0, 3)], r2_sem.at[1])
    done(rb2.at[pl.ds(0, 3)], r2_sem.at[3])
    sum_a, sum_b = sa[y], sb[x]
    for d in RING:
        sum_a = sum_a + ra2[(y + d) % 4]
        sum_b = sum_b + rb2[(x + d) % 4]
    dg[0] = sum_a
    dg[1] = sum_b

    done(tg, out_sem)
    done(lab.at[pl.ds(0, T - RT)], lab_sem.at[0])
    done(dn.at[0, :, pl.ds(0, 128), :], hop_sem.at[0])
    done(cotp.at[pl.ds(CUTS[1], T - CUTS[1])], far_sem.at[0])
    done(upr.at[pl.ds(0, 15 * 32)], up_sem.at[0])
    done(ups.at[pl.ds(0, 16)], up_sem.at[2])
    done(dn.at[pl.ds(0, 15)], dn_send)
    done(wf.at[pl.ds(0, 30 * QUARTER)], w_send)
    done(wf.at[pl.ds(0, 15 * HALF)], sib_send)
    done(ra.at[pl.ds(0, 3)], r_sem.at[0])
    done(rb.at[pl.ds(0, 3)], r_sem.at[2])
    done(ra2.at[pl.ds(0, 3)], r2_sem.at[0])
    done(rb2.at[pl.ds(0, 3)], r2_sem.at[2])
    done(upart.at[pl.ds(0, 15 * 8)], u_sem.at[0])

    for g in range(G):
        done(gs.at[pl.ds(0, 13 * RT), group(g)], g_send.at[g])


def settle(tg, val, dg, ug, tg_out, val_out, dg_out, ug_out):
    tg_out[...] = tg[...]
    val_out[...] = val[...]
    dg_out[...] = dg[...]
    ug_out[...] = ug[...]


def rank_orders():
    three, one = np.zeros((2 * K3, 32 * NF), np.float32), np.zeros((A, A), np.float32)
    for a in range(2):
        for r in range(64):
            for d in range(3):
                three[a * K3 + d * 64 + r, (r // 4) * 32 + d * 8 + a * 4 + r % 4] = 1.0
            one[a * 64 + r, (r // 4) * 8 + a * 4 + r % 4] = 1.0
    return three, one


def local(
    tokens,
    cotangent,
    frozen_weight,
    down_factor_table,
    up_factor_table,
    adapter_of_block,
    block_destination,
    adapter_table_row,
):
    blocks = tokens.shape[0]
    steps = jnp.arange(blocks, dtype=jnp.int32)
    wide = jnp.arange(T, dtype=jnp.int32)
    dest_rep = block_destination // blocks
    slot = block_destination % blocks
    row = jnp.sum(
        jnp.where(adapter_of_block[:, None] == steps[None, :], adapter_table_row[None, :], 0), axis=1
    )
    adapter = row - dest_rep * 2
    before = (dest_rep[:, None] == dest_rep[None, :]) & (steps[None, :] < steps[:, None])
    place = dest_rep * 2 + jnp.sum(before.astype(jnp.int32), axis=1)
    hit = place[None, :] == steps[:, None]
    slot_at = jnp.sum(jnp.where(hit, slot[None, :], 0), axis=1)
    adapter_at = jnp.sum(jnp.where(hit, adapter[None, :], 0), axis=1)

    def by_token(v):
        return jnp.broadcast_to(v[:, None], (blocks, 8)).reshape(T)

    code = by_token(place) * 8 + wide % 8
    slot_code = by_token(slot_at) * 8 + wide % 8
    sel = (wide[:, None] == code[None, :]).astype(bf16)
    selt = (code[:, None] == wide[None, :]).astype(bf16)
    lab = jnp.concatenate(
        [
            (slot_code[:, None] == wide[None, :]).astype(bf16),
            jnp.broadcast_to(by_token(adapter_at)[:, None], (T, A)).astype(bf16),
        ],
        axis=1,
    )
    q, q8 = (jnp.asarray(v, bf16) for v in rank_orders())

    vm = pl.BlockSpec(memory_space=pltpu.VMEM)
    hbm = pl.BlockSpec(memory_space=pl.ANY)
    dma = pltpu.SemaphoreType.DMA
    tg, val, dg, ug = pl.pallas_call(
        kernel,
        out_shape=(
            jax.ShapeDtypeStruct((T, D), bf16),
            jax.ShapeDtypeStruct((T, V), bf16),
            jax.ShapeDtypeStruct((2, 64, DS), f32),
            jax.ShapeDtypeStruct((2, 4, V), f32),
        ),
        in_specs=[hbm, vm, hbm, hbm, vm, vm, vm, vm, vm, vm],
        out_specs=(hbm, vm, vm, vm),
        scratch_shapes=[
            pltpu.VMEM((T, D), bf16),
            pltpu.VMEM((T, D), bf16),
            pltpu.VMEM((T, D), bf16),
            pltpu.VMEM((T, D), bf16),
            pltpu.VMEM((D, V), bf16),
            pltpu.VMEM((NF, 2, K3, DS), bf16),
            pltpu.VMEM((32, V), f32),
            pltpu.VMEM((32, V), bf16),
            pltpu.VMEM((32 * NF, V), bf16),
            pltpu.VMEM((T, T + A), bf16),
            pltpu.VMEM((NF, A, DS), f32),
            pltpu.VMEM((4, 4, 64, DS), f32),
            pltpu.VMEM((4, 4, 64, DS), f32),
            pltpu.VMEM((4, 64, DS), f32),
            pltpu.VMEM((4, 64, DS), f32),
            pltpu.VMEM((4, 64, DS), f32),
            pltpu.VMEM((4, 64, DS), f32),
            pltpu.VMEM((A, V), f32),
            pltpu.VMEM((NF, 8, V), f32),
            pltpu.VMEM((T, V + A), bf16),
            pltpu.VMEM((T, V + A), bf16),
            pltpu.VMEM((T, 4 * K3), bf16),
            pltpu.VMEM((2 * A, T), bf16),
            pltpu.VMEM((2 * K3, V), bf16),
            pltpu.VMEM((T, V), f32),
            pltpu.VMEM((T, A), f32),
            dma((G,)),
            dma((G,)),
            dma((G,)),
            dma((2,)),
            dma((3,)),
            dma,
            dma((5,)),
            dma,
            dma((NF, 2)),
            dma,
            dma,
            dma((NF, 2)),
            dma,
            dma((NF,)),
            dma((3,)),
            dma((G,)),
            dma((G,)),
            dma((4,)),
            dma((4,)),
            dma((2,)),
            dma,
        ],
        compiler_params=pltpu.CompilerParams(
            collective_id=0, has_side_effects=True, vmem_limit_bytes=60 * 1024 * 1024
        ),
        cost_estimate=pl.CostEstimate(
            flops=14 * 10**9, bytes_accessed=12 * 2**20, transcendentals=0
        ),
        name="lora_moves",
    )(
        tokens.reshape(T, D),
        cotangent.reshape(T, V),
        frozen_weight,
        down_factor_table,
        up_factor_table,
        sel,
        selt,
        lab,
        q,
        q8,
    )
    pieces = [
        pl.BlockSpec((blocks // 8, 8, D), lambda i: (i, 0, 0)),
        pl.BlockSpec((blocks // 8, 8, V), lambda i: (i, 0, 0)),
        pl.BlockSpec((2, 8, DS), lambda i: (0, i, 0)),
        pl.BlockSpec((2, 4, V // 8), lambda i: (0, 0, i)),
    ]
    results = (tg.reshape(blocks, 8, D), val.reshape(blocks, 8, V), dg, ug)
    tg, val, dg, ug = pl.pallas_call(
        settle,
        out_shape=tuple(jax.ShapeDtypeStruct(v.shape, v.dtype) for v in results),
        grid=(8,),
        in_specs=pieces,
        out_specs=tuple(pieces),
        name="settle",
    )(*results)
    return val, tg, dg, ug


def solution(mesh):
    placed = (
        P("rep", "fsdp", None),
        P("rep", "fsdp", None),
        P("fsdp", None),
        P("rep", None, "fsdp"),
        P("rep", "fsdp", None),
        P("rep"),
        P("rep"),
        P(),
    )
    return jax.shard_map(
        local,
        mesh=mesh,
        in_specs=placed,
        out_specs=(
            P("rep", "fsdp", None),
            P("rep", "fsdp", None),
            P("rep", None, "fsdp"),
            P("rep", "fsdp", None),
        ),
        check_vma=False,
    )
```

```python
import functools

import jax
import jax.numpy as jnp
import numpy as np
from jax import lax
from jax.experimental import pallas as pl
from jax.experimental.pallas import tpu as pltpu
from jax.sharding import PartitionSpec as P

MESH = pl.DeviceIdType.MESH
bf16, f32 = jnp.bfloat16, jnp.float32

NR = 16
NF = 16
T = 256
RT = T // NR
D = 8192
V = 1024
DS = D // NF
HALF = DS // 2
QUARTER = HALF // 2
A = 128
G = 4
GC = D // G

REPS = [(dz, dc) for dz in (4, 3, 5, 2, 6, 1, 7) for dc in (0, 1)] + [(0, 1)]
RING = (1, 3, 2)
STEPS = (
    (),
    (
        ((1, 0), ((1, 0), (0, 1), (0, -1))),
        ((3, 0), ((0, 1), (0, -1))),
        ((0, 1), ((0, 1),)),
    ),
    (
        ((2, 0), ((0, 1), (0, -1))),
        ((1, 3), ((0, -1),)),
        ((3, 3), ((0, -1),)),
    ),
    (((2, 1), ((0, 1),)),),
)
PASSED = frozenset(off for step in STEPS for off, _ in step)


def nt(a, b):
    return lax.dot_general(a, b, (((1,), (1,)), ((), ())), preferred_element_type=f32)


def tn(a, b):
    return lax.dot_general(a, b, (((0,), (0,)), ((), ())), preferred_element_type=f32)


def nn(a, b):
    return jnp.dot(a, b, preferred_element_type=f32)


def split(v):
    hi = v.astype(bf16)
    return hi, (v - hi.astype(f32)).astype(bf16)


ORDER = {0: 0, 1: 2, 7: 4, 3: 6, 2: 8, 5: 11, 6: 13}
OPPOSITE = (10, 15)
CUTS = (0, 96, 176, 256)
K3 = 192


def arrival_group(dz, dc, c):
    above = -dz % 8
    if above == 4:
        return OPPOSITE[0] + c * (OPPOSITE[1] - OPPOSITE[0])
    return ORDER[above] + dc


def kernel(
    tok, cot, w, down, up, sel, selt, lab, q, q8,
    tg, val, dg, ug,
    xs, xr, gs, gr, wf, dn, ups, upc, upr, labr, dpart, ra, rb, sa, sb, ra2, rb2, upart, urecv,
    cotp, hc, hg, gtcat, upb, acc, mid,
    tok_sem, x_send, x_recv, lab_sem, hop_sem, hop_own, up_sem, dn_send, dn_recv, w_own, w_send, w_recv,
    sib_send, sib_recv, far_sem, g_send, g_recv, r_sem, r2_sem, u_sem, out_sem,
):
    rep, fs = lax.axis_index("rep"), lax.axis_index("fsdp")
    z, c, x, y = rep // 2, rep % 2, fs // 4, fs % 4
    plane = [((x + dx) % 4) * 4 + (y + dy) % 4 for dx in range(4) for dy in range(4)][1:]
    reps = [((z + dz) % 8) * 2 + (c + dc) % 2 for dz, dc in REPS]
    sib = rep + 1 - 2 * c
    above, below = ((z + 3) % 8) * 2 + c, ((z + 5) % 8) * 2 + c

    barrier = pltpu.get_barrier_semaphore()
    for r in reps:
        pl.semaphore_signal(barrier, inc=1, device_id=(r, fs), device_id_type=MESH)
    for f in plane:
        pl.semaphore_signal(barrier, inc=1, device_id=(rep, f), device_id_type=MESH)

    def group(g):
        return pl.ds(pl.multiple_of(g * GC, GC), GC)

    def loads(g):
        return pltpu.make_async_copy(tok.at[:, group(g)], gs.at[:, group(g)], tok_sem.at[g])

    for g in range(G):
        loads(g).start()
    own_w = pltpu.make_async_copy(w, wf.at[pl.ds(pl.multiple_of(fs * DS, DS), DS)], w_own)
    own_w.start()
    own_down = pltpu.make_async_copy(down, dn.at[fs, :, pl.ds(0, 64), :], hop_own)
    own_down.start()
    for a in range(2):
        ups[4 * a : 4 * a + 4, :] = up[a].astype(f32)
    ups[24:, :] = jnp.zeros((8, V), f32)

    for g in range(G):
        loads(g).wait()
        xs[:, group(g)] = nn(sel[...], gs[:, group(g)]).astype(bf16)
    pl.semaphore_wait(barrier, len(reps) + len(plane))

    def rows(r):
        return pl.ds(pl.multiple_of(r * RT, RT), RT)

    def push(src, dst, send, recv, r, f):
        pltpu.make_async_remote_copy(
            src_ref=src, dst_ref=dst, send_sem=send, recv_sem=recv,
            device_id=(r, f), device_id_type=MESH,
        ).start()

    def done(ref, sem):
        pltpu.make_async_copy(ref, ref, sem).wait()

    for (dz, dc), r in zip(REPS, reps):
        push(lab.at[rows(r)], labr.at[rows(arrival_group(dz, dc, c))], lab_sem.at[0], lab_sem.at[1], r, fs)
    pltpu.make_async_copy(lab.at[rows(rep)], labr.at[pl.ds(0, RT)], lab_sem.at[1]).start()
    for k, r in ((1, above), (2, below)):
        push(ups.at[pl.ds(0, 8)], ups.at[pl.ds(8 * k, 8)], up_sem.at[2], up_sem.at[2 + k], r, fs)
        push(down, dn.at[fs, :, pl.ds(64 * k, 64), :], hop_sem.at[0], hop_sem.at[k], r, fs)

    def wpart(f, h, core):
        return wf.at[pl.ds(pl.multiple_of(f * DS + core * HALF + h * QUARTER, QUARTER), QUARTER)]

    def push_w(f, h, to):
        push(wpart(f, h, c), wpart(f, h, c), w_send, w_recv.at[f, h], rep, to)

    def push_dn(f, h, to):
        push(dn.at[f, h], dn.at[f, h], dn_send, dn_recv.at[f, h], rep, to)

    def at(dx, dy):
        return ((x + dx + 4) % 4) * 4 + (y + dy + 4) % 4

    def source(off):
        return at(-off[0], -off[1])

    def ring(own_or, send):
        if own_or == 0:
            for d in (1, -1):
                send(source((0, 0)), 0, at(d, 0))
                send(source((0, 0)), 1, at(0, d))
            for d in (1, -1):
                send(source((0, 0)), 0, at(0, d))
                send(source((0, 0)), 1, at(d, 0))
        for off, goes in STEPS[own_or]:
            for h in (0, 1):
                o = off if h == 0 else off[::-1]
                ref, sem = unit(send, source(o), h)
                done(ref, sem)
                for to in goes:
                    t = to if h == 0 else to[::-1]
                    send(source(o), h, at(*t))

    def unit(send, f, h):
        if send is push_w:
            return wpart(f, h, c), w_recv.at[f, h]
        return dn.at[f, h], dn_recv.at[f, h]

    own_w.wait()
    ring(0, push_w)

    def tokens_off(g):
        for (dz, dc), r in zip(REPS, reps):
            push(
                xs.at[rows(r), group(g)], xr.at[rows(arrival_group(dz, dc, c)), group(g)],
                x_send.at[g], x_recv.at[g], r, fs,
            )
        pltpu.make_async_copy(
            xs.at[rows(rep), group(g)], xr.at[pl.ds(0, RT), group(g)], x_recv.at[g]
        ).start()

    tokens_off(0)

    done(labr, lab_sem.at[1])
    cotp[:, :V] = nn(labr[:, :T], cot[...]).astype(bf16)
    cotp[:, V:] = labr[:, T:]
    served = [pl.ds(CUTS[k], CUTS[k + 1] - CUTS[k]) for k in range(3)]
    for k, r in ((1, above), (2, below)):
        push(cotp.at[served[k]], hc.at[served[k]], far_sem.at[0], far_sem.at[k], r, fs)
    hc[served[0], :] = cotp[served[0], :]
    tokens_off(1)

    done(ups.at[pl.ds(0, 8)], up_sem.at[3])
    done(ups.at[pl.ds(0, 8)], up_sem.at[4])
    upc[...] = ups[...].astype(bf16)
    mine32 = pl.ds(pl.multiple_of(fs * 32, 32), 32)
    for f in plane:
        push(upc, upr.at[mine32], up_sem.at[0], up_sem.at[1], rep, f)
    upr[mine32, :] = upc[...]
    own_down.wait()
    done(down, hop_sem.at[1])
    done(down, hop_sem.at[2])
    ring(0, push_dn)
    tokens_off(2)
    tokens_off(3)

    done(upr.at[pl.ds(0, 15 * 32)], up_sem.at[1])
    upb[...] = nn(q[...], upr[...]).astype(bf16)
    own_up = jnp.concatenate([upb[:64, :], upb[K3 : K3 + 64, :]], axis=0)
    ids = cotp[:, V:].astype(f32)
    mask = jnp.where(lax.broadcasted_iota(jnp.int32, (T, A), 1) < 64, 1.0 - ids, ids)
    hi, lo = split((2.0 * nt(cotp[:, :V], own_up) * mask).T)
    gtcat[:A, :] = hi
    gtcat[A:, :] = lo
    done(hc.at[served[1]], far_sem.at[1])
    done(hc.at[served[2]], far_sem.at[2])
    lane = lax.broadcasted_iota(jnp.int32, (T, 2 * K3), 1)
    row = lax.broadcasted_iota(jnp.int32, (T, 2 * K3), 0)
    owner_at = jnp.where(row >= CUTS[2], 2, jnp.where(row >= CUTS[1], 1, 0))
    ids = hc[:, V:].astype(f32)
    ids = jnp.concatenate([ids, ids, ids], axis=1)
    chosen = jnp.where(lane < K3, 1.0 - ids, ids)
    lane = jnp.where(lane < K3, lane, lane - K3)
    at_lane = jnp.where(lane >= 128, 2, jnp.where(lane >= 64, 1, 0))
    back = jnp.where(at_lane == owner_at, 2.0 * nt(hc[:, :V], upb[...]) * chosen, 0.0)
    hi, lo = split(back)
    hg[:, : 2 * K3] = hi
    hg[:, 2 * K3 :] = lo

    def dcols(f):
        return pl.ds(pl.multiple_of(f * DS, DS), DS)

    back_to = []
    for dc in (0, 1):
        core = (c + dc) % 2
        for k, dz, place in (
            (0, 0, rep), (2, 1, rep), (4, 7, rep), (6, 0, below), (8, 7, below), (11, 0, above), (13, 1, above),
        ):
            back_to.append((k + dc, ((z + dz) % 8) * 2 + core, place))
    back_to.append((OPPOSITE[0], ((z + 1) % 8) * 2, below))
    back_to.append((OPPOSITE[1], ((z + 7) % 8) * 2 + 1, above))
    remote = [e for e in back_to if e[0] not in (0, 6, 11)]
    remote = remote[::-1]

    def grads(f):
        dv = dn[f].reshape(2 * K3, DS)
        out = nt(hc[:, :V], wf[dcols(f), :])
        out = out + nn(hg[:, : 2 * K3], dv) + nn(hg[:, 2 * K3 :], dv)
        gs[:, dcols(f)] = out.astype(bf16)

    def grads_off(g):
        for k, r, place in remote:
            push(
                gs.at[pl.ds(k * RT, RT), group(g)], gr.at[rows(place), group(g)],
                g_send.at[g], g_recv.at[g], r, fs,
            )
        for k, place in ((0, rep), (6, below), (11, above)):
            pltpu.make_async_copy(
                gs.at[pl.ds(k * RT, RT), group(g)], gr.at[rows(place), group(g)], g_recv.at[g]
            ).start()

    def whalf(f, core):
        return wf.at[pl.ds(pl.multiple_of(f * DS + core * HALF, HALF), HALF)]

    def take_in(offs):
        for off in offs:
            f = source(off)
            for h in (0, 1):
                if (off if h == 0 else off[::-1]) not in PASSED:
                    done(wpart(f, h, c), w_recv.at[f, h])
                    done(dn.at[f, h], dn_recv.at[f, h])
            push(whalf(f, c), whalf(f, c), sib_send, sib_recv.at[f], sib, fs)

    def grads_of(count, dx, dy):
        def step(i, _):
            f = ((x + 4 - dx(i)) % 4) * 4 + (y + 4 - dy(i)) % 4
            done(whalf(f, 1 - c), sib_recv.at[f])
            grads(f)
            return 0

        lax.fori_loop(0, count, step, 0)

    def down_terms(g):
        def term(k, _):
            fy = (y + k) % 4
            f = g * 4 + fy
            part = nn(gtcat[...], xr[:, dcols(f)])
            dpart[f] = part[:A] + part[A:]

            @pl.when(g != x)
            def _():
                push(dpart.at[f, pl.ds(0, 64)], ra.at[x, fy], r_sem.at[0], r_sem.at[1], rep, g * 4 + y)

            @pl.when(fy != y)
            def _():
                push(dpart.at[f, pl.ds(64, 64)], rb.at[y, g], r_sem.at[2], r_sem.at[3], rep, x * 4 + fy)

            return 0

        lax.fori_loop(0, 4, term, 0)

    def odd(i):
        return 1 + 2 * (i % 2)

    ring(1, push_w)
    ring(1, push_dn)
    take_in([(1, 0), (3, 0), (0, 1), (0, 3)])
    grads(fs)
    grads_of(4, lambda i: odd(i) * (1 - i // 2), lambda i: odd(i) * (i // 2))
    ring(2, push_w)
    ring(2, push_dn)
    take_in([(2, 0), (0, 2), (1, 1), (3, 1), (1, 3), (3, 3)])
    grads_of(2, lambda i: 2 - 2 * i, lambda i: 2 * i)
    ring(3, push_w)
    ring(3, push_dn)
    grads_of(4, lambda i: odd(i), lambda i: 1 + 2 * (i // 2))
    take_in([(2, 1), (2, 3), (1, 2), (3, 2), (2, 2)])
    grads_of(4, lambda i: 2 - (1 - 2 * (i % 2)) * (i // 2), lambda i: odd(i) + (2 - odd(i)) * (i // 2))
    grads_of(1, lambda i: 2, lambda i: 2)

    def arrived(g, _):
        done(xr.at[:, group(g)], x_recv.at[g])
        down_terms(g)

        @pl.when(g + 1 < G)
        def _():
            grads_off(g + 1)

        return 0

    grads_off(0)
    lax.fori_loop(0, G, arrived, 0)

    acc[...] = jnp.zeros_like(acc)
    mid[...] = jnp.zeros_like(mid)

    def fwd(g, _):
        acc[...] += nn(xr[:, group(g)], wf[group(g), :])
        return 0

    def low(f, _):
        mid[...] += nt(xr[:, dcols(f)], dn[f, :, pl.ds(0, 64), :].reshape(A, DS))
        return 0

    lax.fori_loop(0, G, fwd, 0)
    lax.fori_loop(0, NF, low, 0)

    m2 = 2.0 * mid[...] * mask
    hi, lo = split(m2)
    out = acc[...] + nn(hi, own_up) + nn(lo, own_up)
    val[...] = tn(labr[:, :T], out.astype(bf16)).astype(bf16)
    hi, lo = split(m2.T)
    hi = tn(q8[...], hi).astype(bf16)
    lo = tn(q8[...], lo).astype(bf16)
    own_cot = cotp[:, :V]
    upart[...] = nn(hi, own_cot) + nn(lo, own_cot)
    for f in plane:
        push(upart.at[pl.ds(pl.multiple_of(f * 8, 8), 8)], urecv.at[fs], u_sem.at[0], u_sem.at[1], rep, f)
    mine8 = pl.ds(pl.multiple_of(fs * 8, 8), 8)
    pltpu.make_async_copy(upart.at[mine8], urecv.at[fs], u_sem.at[1]).start()

    done(ra.at[pl.ds(0, 3)], r_sem.at[1])
    done(rb.at[pl.ds(0, 3)], r_sem.at[3])

    def first_sum(k, _):
        own_a, own_b = dpart[x * 4 + k, :64, :], dpart[k * 4 + y, 64:, :]
        for d in RING:
            own_a = own_a + ra[(x + d) % 4, k]
            own_b = own_b + rb[(y + d) % 4, k]
        sa[k] = own_a
        sb[k] = own_b

        @pl.when(k != y)
        def _():
            push(sa.at[k], ra2.at[y], r2_sem.at[0], r2_sem.at[1], rep, x * 4 + k)

        @pl.when(k != x)
        def _():
            push(sb.at[k], rb2.at[x], r2_sem.at[2], r2_sem.at[3], rep, k * 4 + y)

        return 0

    lax.fori_loop(0, 4, first_sum, 0)

    for g in range(G):
        done(xs.at[pl.ds(0, T - RT), group(g)], x_send.at[g])

    def finish(g, _):
        done(gr.at[:, group(g)], g_recv.at[g])
        xs[:, group(g)] = nn(selt[...], gr[:, group(g)]).astype(bf16)
        pltpu.make_async_copy(xs.at[:, group(g)], tg.at[:, group(g)], out_sem).start()
        return 0

    lax.fori_loop(0, G, finish, 0)

    done(urecv, u_sem.at[1])
    up_total = jnp.sum(urecv[...], axis=0)
    for a in range(2):
        ug[a] = up_total[4 * a : 4 * a + 4]
    done(ra2.at[pl.ds(0, 3)], r2_sem.at[1])
    done(rb2.at[pl.ds(0, 3)], r2_sem.at[3])
    sum_a, sum_b = sa[y], sb[x]
    for d in RING:
        sum_a = sum_a + ra2[(y + d) % 4]
        sum_b = sum_b + rb2[(x + d) % 4]
    dg[0] = sum_a
    dg[1] = sum_b

    done(tg, out_sem)
    done(lab.at[pl.ds(0, T - RT)], lab_sem.at[0])
    done(dn.at[0, :, pl.ds(0, 128), :], hop_sem.at[0])
    done(cotp.at[pl.ds(CUTS[1], T - CUTS[1])], far_sem.at[0])
    done(upr.at[pl.ds(0, 15 * 32)], up_sem.at[0])
    done(ups.at[pl.ds(0, 16)], up_sem.at[2])
    done(dn.at[pl.ds(0, 15)], dn_send)
    done(wf.at[pl.ds(0, 30 * QUARTER)], w_send)
    done(wf.at[pl.ds(0, 15 * HALF)], sib_send)
    done(ra.at[pl.ds(0, 3)], r_sem.at[0])
    done(rb.at[pl.ds(0, 3)], r_sem.at[2])
    done(ra2.at[pl.ds(0, 3)], r2_sem.at[0])
    done(rb2.at[pl.ds(0, 3)], r2_sem.at[2])
    done(upart.at[pl.ds(0, 15 * 8)], u_sem.at[0])

    for g in range(G):
        done(gs.at[pl.ds(0, 13 * RT), group(g)], g_send.at[g])


def settle(tg, val, dg, ug, tg_out, val_out, dg_out, ug_out):
    tg_out[...] = tg[...]
    val_out[...] = val[...]
    dg_out[...] = dg[...]
    ug_out[...] = ug[...]


def rank_orders():
    three, one = np.zeros((2 * K3, 32 * NF), np.float32), np.zeros((A, A), np.float32)
    for a in range(2):
        for r in range(64):
            for d in range(3):
                three[a * K3 + d * 64 + r, (r // 4) * 32 + d * 8 + a * 4 + r % 4] = 1.0
            one[a * 64 + r, (r // 4) * 8 + a * 4 + r % 4] = 1.0
    return three, one


def local(
    tokens,
    cotangent,
    frozen_weight,
    down_factor_table,
    up_factor_table,
    adapter_of_block,
    block_destination,
    adapter_table_row,
):
    blocks = tokens.shape[0]
    steps = jnp.arange(blocks, dtype=jnp.int32)
    wide = jnp.arange(T, dtype=jnp.int32)
    dest_rep = block_destination // blocks
    slot = block_destination % blocks
    row = jnp.sum(
        jnp.where(adapter_of_block[:, None] == steps[None, :], adapter_table_row[None, :], 0), axis=1
    )
    adapter = row - dest_rep * 2
    before = (dest_rep[:, None] == dest_rep[None, :]) & (steps[None, :] < steps[:, None])
    place = dest_rep * 2 + jnp.sum(before.astype(jnp.int32), axis=1)
    hit = place[None, :] == steps[:, None]
    slot_at = jnp.sum(jnp.where(hit, slot[None, :], 0), axis=1)
    adapter_at = jnp.sum(jnp.where(hit, adapter[None, :], 0), axis=1)

    def by_token(v):
        return jnp.broadcast_to(v[:, None], (blocks, 8)).reshape(T)

    code = by_token(place) * 8 + wide % 8
    slot_code = by_token(slot_at) * 8 + wide % 8
    sel = (wide[:, None] == code[None, :]).astype(bf16)
    selt = (code[:, None] == wide[None, :]).astype(bf16)
    lab = jnp.concatenate(
        [
            (slot_code[:, None] == wide[None, :]).astype(bf16),
            jnp.broadcast_to(by_token(adapter_at)[:, None], (T, A)).astype(bf16),
        ],
        axis=1,
    )
    q, q8 = (jnp.asarray(v, bf16) for v in rank_orders())

    vm = pl.BlockSpec(memory_space=pltpu.VMEM)
    hbm = pl.BlockSpec(memory_space=pl.ANY)
    dma = pltpu.SemaphoreType.DMA
    tg, val, dg, ug = pl.pallas_call(
        kernel,
        out_shape=(
            jax.ShapeDtypeStruct((T, D), bf16),
            jax.ShapeDtypeStruct((T, V), bf16),
            jax.ShapeDtypeStruct((2, 64, DS), f32),
            jax.ShapeDtypeStruct((2, 4, V), f32),
        ),
        in_specs=[hbm, vm, hbm, hbm, vm, vm, vm, vm, vm, vm],
        out_specs=(hbm, vm, vm, vm),
        scratch_shapes=[
            pltpu.VMEM((T, D), bf16),
            pltpu.VMEM((T, D), bf16),
            pltpu.VMEM((T, D), bf16),
            pltpu.VMEM((T, D), bf16),
            pltpu.VMEM((D, V), bf16),
            pltpu.VMEM((NF, 2, K3, DS), bf16),
            pltpu.VMEM((32, V), f32),
            pltpu.VMEM((32, V), bf16),
            pltpu.VMEM((32 * NF, V), bf16),
            pltpu.VMEM((T, T + A), bf16),
            pltpu.VMEM((NF, A, DS), f32),
            pltpu.VMEM((4, 4, 64, DS), f32),
            pltpu.VMEM((4, 4, 64, DS), f32),
            pltpu.VMEM((4, 64, DS), f32),
            pltpu.VMEM((4, 64, DS), f32),
            pltpu.VMEM((4, 64, DS), f32),
            pltpu.VMEM((4, 64, DS), f32),
            pltpu.VMEM((A, V), f32),
            pltpu.VMEM((NF, 8, V), f32),
            pltpu.VMEM((T, V + A), bf16),
            pltpu.VMEM((T, V + A), bf16),
            pltpu.VMEM((T, 4 * K3), bf16),
            pltpu.VMEM((2 * A, T), bf16),
            pltpu.VMEM((2 * K3, V), bf16),
            pltpu.VMEM((T, V), f32),
            pltpu.VMEM((T, A), f32),
            dma((G,)),
            dma((G,)),
            dma((G,)),
            dma((2,)),
            dma((3,)),
            dma,
            dma((5,)),
            dma,
            dma((NF, 2)),
            dma,
            dma,
            dma((NF, 2)),
            dma,
            dma((NF,)),
            dma((3,)),
            dma((G,)),
            dma((G,)),
            dma((4,)),
            dma((4,)),
            dma((2,)),
            dma,
        ],
        compiler_params=pltpu.CompilerParams(
            collective_id=0, has_side_effects=True, vmem_limit_bytes=60 * 1024 * 1024
        ),
        cost_estimate=pl.CostEstimate(
            flops=14 * 10**9, bytes_accessed=12 * 2**20, transcendentals=0
        ),
        name="lora_moves",
    )(
        tokens.reshape(T, D),
        cotangent.reshape(T, V),
        frozen_weight,
        down_factor_table,
        up_factor_table,
        sel,
        selt,
        lab,
        q,
        q8,
    )
    pieces = [
        pl.BlockSpec((blocks // 2, 8, D), lambda i: (i, 0, 0)),
        pl.BlockSpec((blocks // 2, 8, V), lambda i: (i, 0, 0)),
        pl.BlockSpec((2, 32, DS), lambda i: (0, i, 0)),
        pl.BlockSpec((2, 4, V // 2), lambda i: (0, 0, i)),
    ]
    results = (tg.reshape(blocks, 8, D), val.reshape(blocks, 8, V), dg, ug)
    tg, val, dg, ug = pl.pallas_call(
        settle,
        out_shape=tuple(jax.ShapeDtypeStruct(v.shape, v.dtype) for v in results),
        grid=(2,),
        in_specs=pieces,
        out_specs=tuple(pieces),
        name="settle",
    )(*results)
    return val, tg, dg, ug


def solution(mesh):
    placed = (
        P("rep", "fsdp", None),
        P("rep", "fsdp", None),
        P("fsdp", None),
        P("rep", None, "fsdp"),
        P("rep", "fsdp", None),
        P("rep"),
        P("rep"),
        P(),
    )
    return jax.shard_map(
        local,
        mesh=mesh,
        in_specs=placed,
        out_specs=(
            P("rep", "fsdp", None),
            P("rep", "fsdp", None),
            P("rep", None, "fsdp"),
            P("rep", "fsdp", None),
        ),
        check_vma=False,
    )
```
